512 devices in a mesh: gx: 32 (over x_lo, y, core), gy: 16 (over z, x_hi).
Axes of the slice: x: 4 (x_hi: 2, x_lo: 2; x = x_hi * 2 + x_lo), y: 8, z: 8, core: 2. Of those that a mesh axis runs over, the one named last changes fastest.
Arguments:
- features: bfloat16 [32, 16, 1, 512, 128], P('gx', 'gy'), may hold values from -6 to 6
- occupancy: int32 [32, 16, 1, 512], P('gx', 'gy'), may hold values from 0 to 1, as said below
- neighbours: int32 [32, 16, 1, 27], P('gx', 'gy'), may hold values from 0 to 9, as said below
- weight_sub: bfloat16 [27, 128, 128], replicated, may hold values from -0.109375 to 0.109375
- weight_down: bfloat16 [8, 128, 256], replicated, may hold values from -0.1875 to 0.1875
- cotangent: bfloat16 [32, 16, 1, 64, 256], P('gx', 'gy'), may hold values from -6 to 6
Outputs:
- output: bfloat16 [32, 16, 1, 64, 256], P('gx', 'gy')
- grad_features: bfloat16 [32, 16, 1, 512, 128], P('gx', 'gy')
- grad_sub: float32 [27, 128, 128], replicated
- grad_down: float32 [8, 128, 256], replicated
The draws below stay inside these ranges and needn't reach their ends.
Inputs may be any that keep to these rules, and one draw needn't show every extreme that they name: `occupancy`: 0 or 1; every voxel of an empty slot is 0. `neighbours`: tile (x, y) covers the block cells (2 x + a, 2 y + b, c) with a, b, c in 0 and 1. Its single slot holds one active block of these cells. Entry k of an active block's list names the active block at block offset d_k as r + s, with s that block's slot and r = 3 (dx + 1) + (dy + 1) for its tile's offset (dx, dy); 9 where that cell holds no active block, and everywhere in an empty slot.
All inputs are finite; a program needn't handle non-finite values.
Results may differ from the reference program's by a relative error of at most 0.0049.
Values may be sent and summed in bfloat16 or wider, within the bound.
A program may use at most 64 MiB of HBM per device.

```python
import math
import jax
import jax.numpy as jnp
from jax import lax

C1 = 128
C2 = 256
BS = 8
NB = 1
V = 512
N_GX = 32
N_GY = 16


def layout(key):
    scores = jax.random.randint(jax.random.fold_in(key, 101), (N_GX, N_GY, 8), 0, 1 << 20)
    scores = scores * 8 + jnp.arange(8, dtype=jnp.int32)
    cell_order = jnp.argsort(scores, axis=-1).astype(jnp.int32)
    cell_rank = jnp.argsort(cell_order, axis=-1).astype(jnp.int32)
    filled = jax.random.randint(jax.random.fold_in(key, 102), (N_GX, N_GY, 1), 1, NB + 1)
    fullest = jax.random.randint(jax.random.fold_in(key, 103), (), 0, N_GX * N_GY)
    tile_ids = jnp.arange(N_GX * N_GY, dtype=jnp.int32).reshape(N_GX, N_GY, 1)
    filled = jnp.where(tile_ids == fullest, NB, filled)
    return (cell_order, cell_rank, filled)


def draw_neighbours(key, part):
    cell_order, cell_rank, filled = layout(key)
    slot_of_cell = jnp.where(cell_rank < filled, cell_rank, -1)
    cell_grid = slot_of_cell.reshape(N_GX, N_GY, 2, 2, 2).transpose(0, 2, 1, 3, 4).reshape(2 * N_GX, 2 * N_GY, 2)
    cell_grid = jnp.pad(cell_grid, 1, constant_values=-1)
    cell_ids = cell_order[:, :, :NB]
    tile_x = jnp.arange(N_GX, dtype=jnp.int32).reshape(N_GX, 1, 1, 1)
    tile_y = jnp.arange(N_GY, dtype=jnp.int32).reshape(1, N_GY, 1, 1)
    place_x = tile_x * 2 + (cell_ids // 4)[..., None]
    place_y = tile_y * 2 + (cell_ids // 2 % 2)[..., None]
    place_z = (cell_ids % 2)[..., None]
    offsets = jnp.arange(27, dtype=jnp.int32)
    near_x = place_x + offsets // 9 - 1
    near_y = place_y + offsets // 3 % 3 - 1
    near_z = place_z + offsets % 3 - 1
    found_slot = cell_grid[near_x + 1, near_y + 1, near_z + 1]
    owner_x = (near_x + 2) // 2 - 1
    owner_y = (near_y + 2) // 2 - 1
    relative = (owner_x - tile_x + 1) * 3 + (owner_y - tile_y + 1)
    active = jnp.arange(NB, dtype=jnp.int32).reshape(1, 1, NB, 1) < filled[..., None]
    usable = active & (found_slot >= 0)
    return jnp.where(usable, relative * NB + found_slot, 9 * NB).astype(jnp.int32)


def draw_occupancy(key, part):
    cell_order, cell_rank, filled = layout(key)
    key = jax.random.fold_in(key, 2)
    density = jax.random.randint(jax.random.fold_in(key, 1), (N_GX, N_GY, 1, 1), 15, 91)
    levels = jax.random.randint(jax.random.fold_in(key, 2), (N_GX, N_GY, NB, V), 0, 100)
    active = jnp.arange(NB, dtype=jnp.int32).reshape(1, 1, NB, 1) < filled[..., None]
    return jnp.where(active & (levels < density), 1, 0).astype(jnp.int32)


def block_scale(own_key, shape, split, smallest, top_value):
    def one(axis_at, shards_of):
        steps = jax.random.uniform(jax.random.fold_in(jax.random.fold_in(own_key, 6), axis_at), (shards_of,), jnp.float32, smallest / len(split), top_value / len(split))
        return jnp.repeat(jnp.exp(steps), shape[axis_at] // shards_of).reshape((-1,) + (1,) * (len(shape) - axis_at - 1))

    factor_of = one(*split[0])
    for cut in split[1:]:
        factor_of = factor_of * one(*cut)
    return factor_of


def gaussian(rng, shape, scale, bound, cuts=(), kind=jnp.bfloat16):
    entries = scale * jax.random.normal(rng, shape, jnp.float32)
    if cuts:
        entries = entries * block_scale(rng, shape, cuts, -0.22, 0.18)
    return jnp.clip(entries, -bound, bound).astype(kind)


def setup_inputs(seed: int = 0) -> dict:
    arg_keys = jax.random.split(jax.random.key(seed), 7)
    features = gaussian(arg_keys[0], (N_GX, N_GY, NB, V, C1), 1.0, 6.0, ((0, 32), (1, 16)))
    occupancy = draw_occupancy(jax.random.fold_in(arg_keys[6], 71), 0)
    neighbours = draw_neighbours(jax.random.fold_in(arg_keys[6], 71), 0)
    weight_sub = gaussian(arg_keys[3], (27, C1, C1), (27 * C1) ** -0.5, 0.109375)
    weight_down = gaussian(arg_keys[4], (8, C1, C2), (8 * C1) ** -0.5, 0.1875)
    cotangent = gaussian(arg_keys[5], (N_GX, N_GY, NB, V // 8, C2), 1.0, 6.0, ((0, 32), (1, 16)))
    return dict(features=features, occupancy=occupancy, neighbours=neighbours, weight_sub=weight_sub, weight_down=weight_down, cotangent=cotangent)


def densify(block_pool, near_links):
    extent = block_pool.shape[1]
    source_spans = ((extent - 1, extent), (0, extent), (0, 1))
    planes = []
    for i in range(3):
        slab_rows = []
        for j in range(3):
            strips = []
            for l in range(3):
                region = block_pool[:, source_spans[i][0]:source_spans[i][1], source_spans[j][0]:source_spans[j][1], source_spans[l][0]:source_spans[l][1], :]
                strips.append(jnp.take(region, near_links[:, 9 * i + 3 * j + l], axis=0))
            slab_rows.append(jnp.concatenate(strips, axis=3))
        planes.append(jnp.concatenate(slab_rows, axis=2))
    return jnp.concatenate(planes, axis=1)

def convolve(padded_field, weights):
    extent = padded_field.shape[1] - 2
    channels = padded_field.shape[-1]
    summed = jnp.zeros((padded_field.shape[0] * extent ** 3, weights.shape[2]), jnp.float32)
    for i in range(3):
        for j in range(3):
            for l in range(3):
                window = padded_field[:, i:i + extent, j:j + extent, l:l + extent, :].reshape(-1, channels)
                summed = summed + jnp.dot(window, weights[9 * i + 3 * j + l], preferred_element_type=jnp.float32)
    return summed

def weight_grads(padded_field, preact_grad):
    extent = padded_field.shape[1] - 2
    channels = padded_field.shape[-1]
    terms = []
    for i in range(3):
        for j in range(3):
            for l in range(3):
                window = padded_field[:, i:i + extent, j:j + extent, l:l + extent, :].reshape(-1, channels)
                terms.append(lax.dot_general(window, preact_grad, (((0,), (0,)), ((), ())), preferred_element_type=jnp.float32))
    return jnp.stack(terms)

def with_blank(flat_pool):
    shaped = flat_pool.reshape(flat_pool.shape[0], BS, BS, BS, flat_pool.shape[-1])
    blank_block = jnp.zeros((1, BS, BS, BS, flat_pool.shape[-1]), flat_pool.dtype)
    return jnp.concatenate([shaped, blank_block], axis=0)

def group_children(hidden):
    half = BS // 2
    shaped = hidden.reshape(NB, half, 2, half, 2, half, 2, hidden.shape[-1])
    return jnp.transpose(shaped, (0, 1, 3, 5, 2, 4, 6, 7)).reshape(NB * half ** 3, 8 * hidden.shape[-1])

def spread_children(grouped):
    half = BS // 2
    shaped = grouped.reshape(NB, half, half, half, 2, 2, 2, C1)
    return jnp.transpose(shaped, (0, 1, 4, 2, 5, 3, 6, 7)).reshape(NB * V, C1)

def coarse_mask(occupied):
    half = BS // 2
    return lax.optimization_barrier(jnp.max(occupied.reshape(NB, half, 2, half, 2, half, 2), axis=(2, 4, 6))).reshape(NB * half ** 3, 1)

def reference(features, occupancy, neighbours, weight_sub, weight_down, cotangent):
    masked = features * occupancy[..., None].astype(features.dtype)
    padded = jnp.pad(masked, ((1, 1), (1, 1), (0, 0), (0, 0), (0, 0)))
    down_flat = weight_down.reshape(8 * C1, C2)
    flipped = jnp.transpose(weight_sub[::-1], (0, 2, 1))
    anchor = jnp.zeros((), jnp.int32)
    grad_scale = 1.0 / math.sqrt(N_GX * N_GY * NB * V)

    def tile_pool(source, index):
        tile_x = index // N_GY
        tile_y = index % N_GY
        corner = (tile_x, tile_y, anchor, anchor, anchor)
        flat_pool = lax.dynamic_slice(source, corner, (3, 3, NB, V, C1)).reshape(9 * NB, V, C1)
        return (with_blank(flat_pool), tile_x, tile_y)

    def forward(carry, index):
        block_pool, tile_x, tile_y = tile_pool(padded, index)
        near_links = neighbours[tile_x, tile_y]
        occupied = occupancy[tile_x, tile_y]
        live_mask = occupied.reshape(NB * V, 1).astype(jnp.float32)
        padded_field = densify(block_pool, near_links)
        preact = convolve(padded_field, weight_sub)
        hidden = (jax.nn.silu(preact) * live_mask).astype(jnp.bfloat16)
        grouped = group_children(hidden)
        coarse = coarse_mask(occupied)
        output = (jnp.dot(grouped, down_flat, preferred_element_type=jnp.float32) * coarse.astype(jnp.float32)).astype(jnp.bfloat16)
        seeded = cotangent[tile_x, tile_y].reshape(NB * V // 8, C2) * coarse.astype(cotangent.dtype)
        grad_down = lax.dot_general(grouped, seeded, (((0,), (0,)), ((), ())), preferred_element_type=jnp.float32)
        hidden_grad = spread_children(lax.dot_general(seeded, down_flat, (((1,), (1,)), ((), ())), preferred_element_type=jnp.float32))
        sigmoid_pre = jax.nn.sigmoid(preact)
        slopes = sigmoid_pre * (1.0 + preact * (1.0 - sigmoid_pre))
        preact_grad = (hidden_grad * slopes * live_mask).astype(jnp.bfloat16)
        grad_sub = weight_grads(padded_field, preact_grad)
        carried = (carry[0] + grad_sub, carry[1] + grad_down.reshape(8, C1, C2))
        return (carried, (output.reshape(NB, V // 8, C2), preact_grad.reshape(NB, V, C1)))
    indices = jnp.arange(N_GX * N_GY, dtype=jnp.int32)
    start = (jnp.zeros((27, C1, C1), jnp.float32), jnp.zeros((8, C1, C2), jnp.float32))
    sums, stacked = lax.scan(forward, start, indices)
    output = stacked[0].reshape(N_GX, N_GY, NB, V // 8, C2)
    grads_pad = jnp.pad(stacked[1].reshape(N_GX, N_GY, NB, V, C1), ((1, 1), (1, 1), (0, 0), (0, 0), (0, 0)))

    def backward(index):
        block_pool, tile_x, tile_y = tile_pool(grads_pad, index)
        live_mask = occupancy[tile_x, tile_y].reshape(NB * V, 1).astype(jnp.float32)
        summed = convolve(densify(block_pool, neighbours[tile_x, tile_y]), flipped)
        return (summed * live_mask).astype(jnp.bfloat16).reshape(NB, V, C1)
    grad_features = lax.map(backward, indices).reshape(N_GX, N_GY, NB, V, C1)
    return (output, grad_features, sums[0] * grad_scale, sums[1] * grad_scale)
```

```python
import math

import jax
import jax.numpy as jnp
from jax import lax
from jax.experimental import pallas as pl
from jax.experimental.pallas import tpu as pltpu
from jax.sharding import PartitionSpec as P

MESH = pl.DeviceIdType.MESH
C1 = 128
C2 = 256
V = 512
X_LO, X_HI, RING = 2, 2, 8
NX = X_LO * X_HI

TILES = 344
HALF = TILES // 2
PART1 = 88
PART2 = HALF - PART1
T1 = PART1 // RING
T1S = -(-T1 // RING)
T2 = PART2 // NX
T2S = -(-T2 // RING)

FACES = ((1, 0), (-1, 0), (0, 1), (0, -1))
EDGES = ((1, 1), (1, -1), (-1, 1), (-1, -1))

F32 = jnp.float32
BF16 = jnp.bfloat16


def field_slabs(source, minus, zero, plus):
    place = lax.broadcasted_iota(jnp.int32, (1, 8, C1), 1)
    below = jnp.where(place == 0, minus, zero)
    above = jnp.where(place == 7, plus, zero)
    return (
        pltpu.roll(source, 1, axis=1) * below,
        source * zero,
        pltpu.roll(source, 7, axis=1) * above,
    )


def kernel(
    near_ref, feat_ref, occ_ref, wsub_ref, wdown_ref, cot_ref,
    out_ref, gfeat_ref, gsum_ref,
    mask_ref, shuf_ref, field_ref, cols_ref, wflip_ref, kids_ref,
    sface, sedge, rface, redge,
    g32, g16, rc, s16, r1a, r1b, q1, q2, r2a, r2b, e1, e2, f1, f2,
    hs_sem, hr_sem, c_sem, a1_sem, b1_sem, a2_sem, b2_sem, a3_sem, b3_sem,
    a4_sem, b4_sem, a5_sem, b5_sem, a6_sem, b6_sem,
):
    gx, gy = lax.axis_index("gx"), lax.axis_index("gy")
    core = gx % 2
    y = (gx // 2) % RING
    x = (gy % X_HI) * X_LO + gx // (2 * RING)
    z = gy // X_HI

    def device(px, py, pz, pc):
        return ((px % X_LO) * (2 * RING) + py * 2 + pc, pz * X_HI + px // X_LO)

    pa = jnp.where(core == 0, y, z)
    pb = jnp.where(core == 0, z, y)

    def on_a(p):
        return device(x, jnp.where(core == 0, p, y), jnp.where(core == 0, z, p), core)

    def on_b(p):
        return device(x, jnp.where(core == 0, y, p), jnp.where(core == 0, p, z), core)

    def on_x(p):
        return device(p, y, z, core)

    partner = device(x, y, z, 1 - core)
    tiles_x, tiles_y = 2 * RING * X_LO, RING * X_HI

    def tile_at(dx, dy):
        return ((gx + dx + tiles_x) % tiles_x, (gy + dy + tiles_y) % tiles_y)

    barrier = pltpu.get_barrier_semaphore()

    def greet(target):
        pl.semaphore_signal(barrier, inc=1, device_id=target, device_id_type=MESH)

    for dx, dy in FACES + EDGES:
        greet(tile_at(dx, dy))
    greet(partner)

    def greet_rings(s, carry):
        greet(on_a((pa + s) % RING))
        greet(on_b((pb + s) % RING))
        return carry

    lax.fori_loop(1, RING, greet_rings, 0)

    def greet_x(s, carry):
        greet(on_x((x + s) % NX))
        return carry

    lax.fori_loop(1, NX, greet_x, 0)

    def remote(src, dst, send, recv, target):
        return pltpu.make_async_remote_copy(
            src_ref=src, dst_ref=dst, send_sem=send, recv_sem=recv,
            device_id=target, device_id_type=MESH,
        )

    def halo_copies(which):
        copies = []
        for d, (dx, dy) in enumerate(FACES):
            copies.append(
                remote(sface.at[which, d], rface.at[which, d], hs_sem.at[which, d],
                       hr_sem.at[which, d], tile_at(dx, dy))
            )
        for d, (dx, dy) in enumerate(EDGES):
            copies.append(
                remote(sedge.at[which, d], redge.at[which, d], hs_sem.at[which, 4 + d],
                       hr_sem.at[which, 4 + d], tile_at(dx, dy))
            )
        return copies

    def stage_halo(which, value):
        cells = value.reshape(8, 8, 8, C1)
        side = {1: 7, -1: 0}
        for d, (dx, dy) in enumerate(FACES):
            face = cells[side[dx]] if dx else cells[:, side[dy]]
            sface[which, d] = face.reshape(64, C1).astype(BF16)
        for d, (dx, dy) in enumerate(EDGES):
            edge = cells[side[dx], side[dy]]
            sedge[which, d] = jnp.concatenate([edge, edge], axis=0).astype(BF16)

    def named(dx, dy, d0, d1):
        return [
            jnp.where(near_ref[0, 9 * (d0 + 1) + 3 * (d1 + 1) + l] == 3 * (dx + 1) + dy + 1, 1.0, 0.0)
            for l in range(3)
        ]

    def columns(which, value):
        zero, one = F32(0.0), F32(1.0)
        center = field_slabs(value.reshape(64, 8, C1), zero, one, zero)
        for l in range(3):
            field_ref[l, 1:9, 1:9] = center[l].reshape(8, 8, 8, C1)
        corner = {}

        def add_corner(cx, cy, slabs):
            for l in range(3):
                old = corner.get((cx, cy, l))
                corner[cx, cy, l] = slabs[l] if old is None else old + slabs[l]

        place = {1: 9, -1: 0}
        near_row = {1: 0, -1: 7}
        for dx, dy in FACES:
            slot = FACES.index((-dx, -dy))
            face = rface[which, slot].astype(F32).reshape(8, 8, C1)
            slabs = field_slabs(face, *named(dx, dy, dx, dy))
            for l in range(3):
                if dx:
                    field_ref[l, place[dx], 1:9] = slabs[l]
                else:
                    for r in range(8):
                        field_ref[l, 1 + r, place[dy]] = slabs[l][r]
            for side in (1, -1):
                row = near_row[side]
                d0, d1 = (dx, side) if dx else (side, dy)
                add_corner(
                    place[d0], place[d1],
                    field_slabs(face[row : row + 1], *named(dx, dy, d0, d1)),
                )
        for dx, dy in EDGES:
            slot = EDGES.index((-dx, -dy))
            edge = redge[which, slot].astype(F32)[0:8].reshape(1, 8, C1)
            add_corner(place[dx], place[dy], field_slabs(edge, *named(dx, dy, dx, dy)))
        for (cx, cy, l), slab in corner.items():
            field_ref[l, cx, cy] = slab[0]
        for i in range(3):
            for j in range(3):
                for l in range(3):
                    k = 9 * i + 3 * j + l
                    window = field_ref[l, i : i + 8, j : j + 8]
                    cols_ref[:, k * C1 : (k + 1) * C1] = window.reshape(V, C1).astype(BF16)

    def split_children(value):
        cells = value.reshape(8, 4, 2, 8, C1)
        for ey in range(2):
            shuf_ref[ey * 256 : (ey + 1) * 256] = cells[:, :, ey].reshape(256, C1)
        children = [None] * 8
        for ey in range(2):
            for ez in range(2):
                half = shuf_ref[pl.ds(ey * 256 + ez, 128, stride=2), :].reshape(4, 2, 16, C1)
                for ex in range(2):
                    children[4 * ex + 2 * ey + ez] = half[:, ex].reshape(64, C1)
        return children

    def join_children(children):
        for ey in range(2):
            for ez in range(2):
                pair = [children[4 * ex + 2 * ey + ez].reshape(4, 1, 16, C1) for ex in range(2)]
                shuf_ref[pl.ds(ey * 256 + ez, 128, stride=2), :] = jnp.concatenate(
                    pair, axis=1
                ).reshape(128, C1)
        sides = [shuf_ref[e * 256 : (e + 1) * 256].reshape(8, 4, 1, 8, C1) for e in range(2)]
        return jnp.concatenate(sides, axis=2).reshape(V, C1)

    for r in range(4):
        line = occ_ref[0:1, r * 128 : (r + 1) * 128].astype(F32)
        mask_ref[r * 128 : (r + 1) * 128] = jnp.broadcast_to(line, (128, 128)).T
    masked = feat_ref[...].astype(F32) * mask_ref[...]
    stage_halo(0, masked)
    pl.semaphore_wait(barrier, 9 + 2 * (RING - 1) + NX - 1)
    halo = halo_copies(0)
    for copy in halo:
        copy.start()

    for k in range(27):
        wflip_ref[:, k * C1 : (k + 1) * C1] = wsub_ref[(26 - k) * C1 : (27 - k) * C1]
    coarse = None
    for child in split_children(mask_ref[...]):
        coarse = child if coarse is None else jnp.maximum(coarse, child)
    coarse = jnp.concatenate([coarse, coarse], axis=1)
    seeded = (cot_ref[...].astype(F32) * coarse).astype(BF16)
    spread = lax.dot_general(
        seeded, wdown_ref[...], (((1,), (1,)), ((), ())), preferred_element_type=F32
    )
    hidden_grad = join_children([spread[:, r * C1 : (r + 1) * C1] for r in range(8)])

    for copy in halo:
        copy.wait_recv()
    columns(0, masked)
    preact = jnp.dot(cols_ref[...], wsub_ref[...], preferred_element_type=F32)
    sig = jax.nn.sigmoid(preact)
    mask = mask_ref[...]
    hidden = (preact * sig * mask).astype(BF16).astype(F32)
    pre_grad = (hidden_grad * (sig * (1.0 + preact * (1.0 - sig))) * mask).astype(BF16).astype(F32)
    stage_halo(1, pre_grad)
    halo2 = halo_copies(1)
    for copy in halo2:
        copy.start()

    for r, child in enumerate(split_children(hidden)):
        kids_ref[:, r * C1 : (r + 1) * C1] = child.astype(BF16)

    def put(tile, value):
        count = value.shape[0] // 16
        value = value.reshape(count, 16, C1)
        g32[tile : tile + count] = value
        g16[tile : tile + count] = value.astype(BF16)

    grad_down = lax.dot_general(
        kids_ref[...], seeded, (((0,), (0,)), ((), ())), preferred_element_type=F32
    )
    put(216, grad_down[:, :C1])
    put(280, grad_down[:, C1:])
    turned = pre_grad.T.astype(BF16)
    for k in range(27):
        block = jnp.dot(
            turned, cols_ref[:, k * C1 : (k + 1) * C1], preferred_element_type=F32
        )
        put(8 * k, block.T)

    mine, theirs = core * HALF, (1 - core) * HALF
    starts = (0, PART1)
    sizes = (PART1, PART2)
    core_copies = [
        remote(g16.at[pl.ds(theirs + starts[p], sizes[p])], rc.at[pl.ds(starts[p], sizes[p])],
               c_sem.at[0, p], c_sem.at[1, p], partner)
        for p in range(2)
    ]
    for copy in core_copies:
        copy.start()

    def ring_copy(s, n, place, where, src, dst, sem):
        return remote(src, dst, sem.at[0, s], sem.at[1, s], where((place + s) % n))

    def start_all(n, make):
        def body(s, carry):
            make(s).start()
            return carry

        lax.fori_loop(1, n, body, 0)

    def recv_all(n, make):
        def body(s, carry):
            make(s).wait_recv()
            return carry

        lax.fori_loop(1, n, body, 0)

    def send_all(n, make):
        def body(s, carry):
            make(s).wait_send()
            return carry

        lax.fori_loop(1, n, body, 0)

    def scatter1a(s):
        return ring_copy(s, RING, pa, on_a, s16.at[pl.ds(((pa + s) % RING) * T1, T1)], r1a.at[s], a1_sem)

    def scatter1b(s):
        return ring_copy(s, NX, x, on_x, s16.at[pl.ds(PART1 + ((x + s) % NX) * T2, T2)], r1b.at[s], b1_sem)

    def scatter2a(s):
        return ring_copy(s, RING, pb, on_b, q1.at[pl.ds(((pb + s) % RING) * T1S, T1S)], r2a.at[s], a2_sem)

    def scatter2b(s):
        return ring_copy(s, RING, pa, on_a, q2.at[pl.ds(((pa + s) % RING) * T2S, T2S)], r2b.at[s], b2_sem)

    def swap3a(s):
        return ring_copy(s, NX, x, on_x, e1.at[x], e1.at[x], a3_sem)

    def swap3b(s):
        return ring_copy(s, RING, pb, on_b, e2.at[pb], e2.at[pb], b3_sem)

    def gather2a(s):
        own = f1.at[pl.ds(pb * T1S, T1S)]
        return ring_copy(s, RING, pb, on_b, own, own, a4_sem)

    def gather2b(s):
        own = f2.at[pl.ds(pa * T2S, T2S)]
        return ring_copy(s, RING, pa, on_a, own, own, b4_sem)

    def piece1(p):
        return gsum_ref.at[pl.ds(mine + p * T1, T1)]

    def piece2(p):
        return gsum_ref.at[pl.ds(mine + PART1 + p * T2, T2)]

    def gather1a(s):
        return ring_copy(s, RING, pa, on_a, piece1(pa), piece1(pa), a5_sem)

    def gather1b(s):
        return ring_copy(s, NX, x, on_x, piece2(x), piece2(x), b5_sem)

    def across_a(s):
        piece = piece1((pa - s + RING) % RING)
        return remote(piece, piece, a6_sem.at[0, s], a6_sem.at[1, s], partner)

    def across_b(s):
        piece = piece2((x - s + NX) % NX)
        return remote(piece, piece, b6_sem.at[0, s], b6_sem.at[1, s], partner)

    def pair_sum(at, count):
        return g32[pl.ds(mine + at, count)] + rc[pl.ds(at, count)].astype(F32)

    core_copies[0].wait_recv()
    s16[0:PART1] = pair_sum(0, PART1).astype(BF16)
    start_all(RING, scatter1a)
    core_copies[1].wait_recv()
    s16[PART1:HALF] = pair_sum(PART1, PART2).astype(BF16)
    start_all(NX, scatter1b)

    for copy in halo2:
        copy.wait_recv()
    columns(1, pre_grad)
    gfeat = lax.dot_general(
        cols_ref[...], wflip_ref[...], (((1,), (1,)), ((), ())), preferred_element_type=F32
    )
    gfeat_ref[...] = (gfeat * mask_ref[...]).astype(BF16)
    output = jnp.dot(kids_ref[...], wdown_ref[...], preferred_element_type=F32)
    out_ref[...] = (output * coarse).astype(BF16)

    recv_all(RING, scatter1a)
    total = pair_sum(pa * T1, T1)
    for s in range(1, RING):
        total = total + r1a[s].astype(F32)
    q1[0:T1] = total.astype(BF16)
    if T1S * RING > T1:
        q1[T1 : T1S * RING] = jnp.zeros((T1S * RING - T1, 16, C1), BF16)
    start_all(RING, scatter2a)

    recv_all(NX, scatter1b)
    total = pair_sum(PART1 + x * T2, T2)
    for s in range(1, NX):
        total = total + r1b[s].astype(F32)
    q2[0:T2] = total.astype(BF16)
    if T2S * RING > T2:
        q2[T2 : T2S * RING] = jnp.zeros((T2S * RING - T2, 16, C1), BF16)
    start_all(RING, scatter2b)

    recv_all(RING, scatter2a)
    total = q1[pl.ds(pb * T1S, T1S)].astype(F32)
    for s in range(1, RING):
        total = total + r2a[s].astype(F32)
    e1[x] = total.astype(BF16)
    start_all(NX, swap3a)

    recv_all(RING, scatter2b)
    total = q2[pl.ds(pa * T2S, T2S)].astype(F32)
    for s in range(1, RING):
        total = total + r2b[s].astype(F32)
    e2[pb] = total.astype(BF16)
    start_all(RING, swap3b)

    recv_all(NX, swap3a)
    total = e1[0].astype(F32)
    for p in range(1, NX):
        total = total + e1[p].astype(F32)
    f1[pl.ds(pb * T1S, T1S)] = total.astype(BF16)
    start_all(RING, gather2a)

    recv_all(RING, swap3b)
    total = e2[0].astype(F32)
    for p in range(1, RING):
        total = total + e2[p].astype(F32)
    f2[pl.ds(pa * T2S, T2S)] = total.astype(BF16)
    start_all(RING, gather2b)

    recv_all(RING, gather2a)
    gsum_ref[pl.ds(mine + pa * T1, T1)] = f1[0:T1]
    start_all(RING, gather1a)
    across_a(0).start()

    recv_all(RING, gather2b)
    gsum_ref[pl.ds(mine + PART1 + x * T2, T2)] = f2[0:T2]
    start_all(NX, gather1b)
    across_b(0).start()

    def pass_a(s, carry):
        gather1a(s).wait_recv()
        across_a(s).start()
        return carry

    def pass_b(s, carry):
        gather1b(s).wait_recv()
        across_b(s).start()
        return carry

    lax.fori_loop(1, NX, pass_b, 0)
    lax.fori_loop(1, RING, pass_a, 0)
    across_b(0).wait_recv()
    recv_all(NX, across_b)
    across_a(0).wait_recv()
    recv_all(RING, across_a)

    for copy in halo + halo2 + core_copies:
        copy.wait_send()
    for make in (scatter1a, scatter2a, scatter2b, swap3b, gather2a, gather2b, gather1a, across_a):
        send_all(RING, make)
    for make in (scatter1b, swap3a, gather1b, across_b):
        send_all(NX, make)
    across_a(0).wait_send()
    across_b(0).wait_send()


def local(features, occupancy, neighbours, weight_sub, weight_down, cotangent):
    def tiles(*shape):
        return pltpu.VMEM(shape + (16, C1), BF16)

    vmem = pl.BlockSpec(memory_space=pltpu.VMEM)
    ring, short = pltpu.SemaphoreType.DMA((2, RING)), pltpu.SemaphoreType.DMA((2, NX))
    output, grad_features, sums = pl.pallas_call(
        kernel,
        out_shape=(
            jax.ShapeDtypeStruct((64, C2), BF16),
            jax.ShapeDtypeStruct((V, C1), BF16),
            jax.ShapeDtypeStruct((TILES, 16, C1), BF16),
        ),
        in_specs=[pl.BlockSpec(memory_space=pltpu.SMEM)] + [vmem] * 5,
        out_specs=(vmem, vmem, vmem),
        scratch_shapes=[
            pltpu.VMEM((V, C1), F32),
            pltpu.VMEM((V, C1), F32),
            pltpu.VMEM((3, 10, 10, 8, C1), F32),
            pltpu.VMEM((V, 27 * C1), BF16),
            pltpu.VMEM((C1, 27 * C1), BF16),
            pltpu.VMEM((64, 8 * C1), BF16),
            pltpu.VMEM((2, 4, 64, C1), BF16),
            pltpu.VMEM((2, 4, 16, C1), BF16),
            pltpu.VMEM((2, 4, 64, C1), BF16),
            pltpu.VMEM((2, 4, 16, C1), BF16),
            pltpu.VMEM((TILES, 16, C1), F32),
            tiles(TILES), tiles(HALF), tiles(HALF),
            tiles(RING, T1), tiles(NX, T2),
            tiles(T1S * RING), tiles(T2S * RING),
            tiles(RING, T1S), tiles(RING, T2S),
            tiles(NX, T1S), tiles(RING, T2S),
            tiles(T1S * RING), tiles(T2S * RING),
            pltpu.SemaphoreType.DMA((2, 8)), pltpu.SemaphoreType.DMA((2, 8)),
            pltpu.SemaphoreType.DMA((2, 2)),
            ring, short, ring, ring, short, ring, ring, ring, ring, short, ring, short,
        ],
        compiler_params=pltpu.CompilerParams(
            collective_id=0, has_side_effects=True, vmem_limit_bytes=48 * 1024 * 1024
        ),
    )(
        neighbours.reshape(1, 27),
        features.reshape(V, C1),
        occupancy.reshape(1, V),
        weight_sub.reshape(27 * C1, C1),
        weight_down.reshape(8 * C1, C2),
        cotangent.reshape(64, C2),
    )
    scale = 1.0 / math.sqrt(lax.axis_size("gx") * lax.axis_size("gy") * V)
    grad_sub = sums[:216].reshape(27, C1, C1).astype(F32) * scale
    grad_down = sums[216:].reshape(2, 8, C1, C1).astype(F32) * scale
    return (
        output.reshape(1, 1, 1, 64, C2),
        grad_features.reshape(1, 1, 1, V, C1),
        grad_sub,
        jnp.concatenate([grad_down[0], grad_down[1]], axis=2),
    )


def solution(mesh):
    return jax.shard_map(
        local,
        mesh=mesh,
        in_specs=(
            P("gx", "gy", None, None, None),
            P("gx", "gy", None, None),
            P("gx", "gy", None, None),
            P(),
            P(),
            P("gx", "gy", None, None, None),
        ),
        out_specs=(P("gx", "gy", None, None, None), P("gx", "gy", None, None, None), P(), P()),
        check_vma=False,
    )
```

```python
import functools
import math

import jax
import jax.numpy as jnp
from jax import lax
from jax.experimental import pallas as pl
from jax.experimental.pallas import tpu as pltpu
from jax.sharding import PartitionSpec as P

MESH = pl.DeviceIdType.MESH
C1 = 128
C2 = 256
V = 512
X_LO, X_HI, RING = 2, 2, 8
NX = X_LO * X_HI

SUB_OWNERS = RING - 1
SUB_T = -(-108 // (NX * SUB_OWNERS))
SUB = NX * SUB_OWNERS * SUB_T
HALF = SUB + 64
ORDER = (2, 1, 3, 0) if NX == 4 else (1, 0)
PARTS = ((SUB, RING, 64 // (NX * RING)), (0, SUB_OWNERS, SUB_T))


FACES = ((1, 0), (-1, 0), (0, 1), (0, -1))
EDGES = ((1, 1), (1, -1), (-1, 1), (-1, -1))

F32 = jnp.float32
BF16 = jnp.bfloat16


def field_slabs(source, minus, zero, plus):
    place = lax.broadcasted_iota(jnp.int32, (1, 8, C1), 1)
    below = jnp.where(place == 0, minus, zero)
    above = jnp.where(place == 7, plus, zero)
    return (
        pltpu.roll(source, 1, axis=1) * below,
        source * zero,
        pltpu.roll(source, 7, axis=1) * above,
    )


def kernel(
    near_in, feat_in, occ_in, wsub_in, wdown_in, cot_in,
    out_ref, gfeat_ref, gsum_ref,
    near_ref, feat_ref, occ_ref, wsub_ref, wdown_ref, cot_ref,
    mask_ref, shuf_ref, field_ref, cols_ref, wflip_ref, kids_ref,
    shalo, rhalo, g32, g16, in_sem, hs_sem, hr_sem, *part_refs,
):
    loads = [
        pltpu.make_async_copy(src, dst, in_sem.at[i])
        for i, (src, dst) in enumerate(
            (
                (occ_in, occ_ref), (feat_in, feat_ref), (near_in, near_ref),
                (wdown_in, wdown_ref), (cot_in, cot_ref), (wsub_in, wsub_ref),
            )
        )
    ]
    for load in loads:
        load.start()
    gx, gy = lax.axis_index("gx"), lax.axis_index("gy")
    core = gx % 2
    y = (gx // 2) % RING
    x = (gy % X_HI) * X_LO + gx // (2 * RING)
    z = gy // X_HI

    def device(px, py, pz, pc):
        return ((px % X_LO) * (2 * RING) + py * 2 + pc, pz * X_HI + px // X_LO)

    pa = jnp.where(core == 0, y, z)
    pb = jnp.where(core == 0, z, y)

    def on_plane(px, p):
        return device(px, jnp.where(core == 0, p, y), jnp.where(core == 0, z, p), core)

    def on_b(p):
        return device(x, jnp.where(core == 0, y, p), jnp.where(core == 0, p, z), core)

    partner = device(x, y, z, 1 - core)
    tiles_x, tiles_y = 2 * RING * X_LO, RING * X_HI

    def tile_at(dx, dy):
        return ((gx + dx + tiles_x) % tiles_x, (gy + dy + tiles_y) % tiles_y)

    barrier = pltpu.get_barrier_semaphore()

    def greet(target):
        pl.semaphore_signal(barrier, inc=1, device_id=target, device_id_type=MESH)

    for dx, dy in FACES + EDGES:
        greet(tile_at(dx, dy))
    greet(partner)

    def greet_plane(i, carry):
        greet(on_plane((x + i // RING) % NX, (pa + i) % RING))
        return carry

    lax.fori_loop(1, NX * RING, greet_plane, 0)

    def greet_ring(s, carry):
        greet(on_b((pb + s) % RING))
        return carry

    lax.fori_loop(1, RING, greet_ring, 0)

    def remote(src, dst, send, recv, target):
        return pltpu.make_async_remote_copy(
            src_ref=src, dst_ref=dst, send_sem=send, recv_sem=recv,
            device_id=target, device_id_type=MESH,
        )

    def send_halo(which):
        for d, (dx, dy) in enumerate(FACES):
            region = pl.ds(4 * d, 4)
            remote(shalo.at[which, region], rhalo.at[which, region], hs_sem.at[which],
                   hr_sem.at[which], tile_at(dx, dy)).start()
        for d, (dx, dy) in enumerate(EDGES):
            region = pl.ds(16 + d, 1)
            remote(shalo.at[which, region], rhalo.at[which, region], hs_sem.at[which],
                   hr_sem.at[which], tile_at(dx, dy)).start()

    def whole_halo(which):
        return remote(shalo.at[which], rhalo.at[which], hs_sem.at[which], hr_sem.at[which], partner)

    def stage_halo(which, value):
        cells = value.reshape(8, 8, 8, C1)
        side = {1: 7, -1: 0}
        for d, (dx, dy) in enumerate(FACES):
            face = cells[side[dx]] if dx else cells[:, side[dy]]
            shalo[which, 4 * d : 4 * d + 4] = face.reshape(4, 16, C1).astype(BF16)
        for d, (dx, dy) in enumerate(EDGES):
            edge = cells[side[dx], side[dy]]
            shalo[which, 16 + d] = jnp.concatenate([edge, edge], axis=0).astype(BF16)

    def named(dx, dy, d0, d1):
        return [
            jnp.where(near_ref[0, 9 * (d0 + 1) + 3 * (d1 + 1) + l] == 3 * (dx + 1) + dy + 1, 1.0, 0.0)
            for l in range(3)
        ]

    def center(value):
        slabs = field_slabs(value.reshape(64, 8, C1), F32(0.0), F32(1.0), F32(0.0))
        for l in range(3):
            field_ref[l, 1:9, 1:9] = slabs[l].reshape(8, 8, 8, C1)

    def columns(which):
        corner = {}

        def add_corner(cx, cy, slabs):
            for l in range(3):
                old = corner.get((cx, cy, l))
                corner[cx, cy, l] = slabs[l] if old is None else old + slabs[l]

        place = {1: 9, -1: 0}
        near_row = {1: 0, -1: 7}
        for dx, dy in FACES:
            slot = FACES.index((-dx, -dy))
            face = rhalo[which, 4 * slot : 4 * slot + 4].astype(F32).reshape(8, 8, C1)
            slabs = field_slabs(face, *named(dx, dy, dx, dy))
            for l in range(3):
                if dx:
                    field_ref[l, place[dx], 1:9] = slabs[l]
                else:
                    for r in range(8):
                        field_ref[l, 1 + r, place[dy]] = slabs[l][r]
            for side in (1, -1):
                row = near_row[side]
                d0, d1 = (dx, side) if dx else (side, dy)
                add_corner(
                    place[d0], place[d1],
                    field_slabs(face[row : row + 1], *named(dx, dy, d0, d1)),
                )
        for dx, dy in EDGES:
            slot = EDGES.index((-dx, -dy))
            edge = rhalo[which, 16 + slot].astype(F32)[0:8].reshape(1, 8, C1)
            add_corner(place[dx], place[dy], field_slabs(edge, *named(dx, dy, dx, dy)))
        for (cx, cy, l), slab in corner.items():
            field_ref[l, cx, cy] = slab[0]
        for i in range(3):
            for j in range(3):
                for l in range(3):
                    k = 9 * i + 3 * j + l
                    window = field_ref[l, i : i + 8, j : j + 8]
                    cols_ref[:, k * C1 : (k + 1) * C1] = window.reshape(V, C1).astype(BF16)

    def split_children(value):
        cells = value.reshape(8, 4, 2, 8, C1)
        for ey in range(2):
            shuf_ref[ey * 256 : (ey + 1) * 256] = cells[:, :, ey].reshape(256, C1)
        children = [None] * 8
        for ey in range(2):
            for ez in range(2):
                half = shuf_ref[pl.ds(ey * 256 + ez, 128, stride=2), :].reshape(4, 2, 16, C1)
                for ex in range(2):
                    children[4 * ex + 2 * ey + ez] = half[:, ex].reshape(64, C1)
        return children

    def join_children(children):
        for ey in range(2):
            for ez in range(2):
                pair = [children[4 * ex + 2 * ey + ez].reshape(4, 1, 16, C1) for ex in range(2)]
                shuf_ref[pl.ds(ey * 256 + ez, 128, stride=2), :] = jnp.concatenate(
                    pair, axis=1
                ).reshape(128, C1)
        sides = [shuf_ref[e * 256 : (e + 1) * 256].reshape(8, 4, 1, 8, C1) for e in range(2)]
        return jnp.concatenate(sides, axis=2).reshape(V, C1)

    loads[0].wait()
    for r in range(4):
        line = occ_ref[0:1, r * 128 : (r + 1) * 128].astype(F32)
        mask_ref[r * 128 : (r + 1) * 128] = jnp.broadcast_to(line, (128, 128)).T
    loads[1].wait()
    masked = feat_ref[...].astype(F32) * mask_ref[...]
    stage_halo(0, masked)
    pl.semaphore_wait(barrier, 9 + NX * RING - 1 + RING - 1)
    send_halo(0)

    center(masked)
    for load in loads[2:]:
        load.wait()
    for k in range(27):
        wflip_ref[:, k * C1 : (k + 1) * C1] = wsub_ref[(26 - k) * C1 : (27 - k) * C1]
    coarse = None
    for child in split_children(mask_ref[...]):
        coarse = child if coarse is None else jnp.maximum(coarse, child)
    coarse = jnp.concatenate([coarse, coarse], axis=1)
    seeded = (cot_ref[...].astype(F32) * coarse).astype(BF16)
    spread = lax.dot_general(
        seeded, wdown_ref[...], (((1,), (1,)), ((), ())), preferred_element_type=F32
    )
    hidden_grad = join_children([spread[:, r * C1 : (r + 1) * C1] for r in range(8)])

    whole_halo(0).wait_recv()
    columns(0)
    preact = jnp.dot(cols_ref[...], wsub_ref[...], preferred_element_type=F32)
    sig = jax.nn.sigmoid(preact)
    mask = mask_ref[...]
    hidden = (preact * sig * mask).astype(BF16).astype(F32)
    for r, child in enumerate(split_children(hidden)):
        kids_ref[:, r * C1 : (r + 1) * C1] = child.astype(BF16)

    mine, theirs = core * HALF, (1 - core) * HALF

    def put(tile, value):
        value = value.reshape(value.shape[0] // 16, 16, C1)
        g32[tile : tile + value.shape[0]] = value
        g16[tile : tile + value.shape[0]] = value.astype(BF16)

    class Part:
        def __init__(self, index):
            self.at, self.owners, self.t = PARTS[index]
            self.group = self.owners * self.t
            self.count = NX * self.group
            (self.rc, self.s16, self.r1, self.e,
             self.send, self.recv, self.late) = part_refs[7 * index : 7 * index + 7]

        def when_owner(self, body):
            if self.owners == RING:
                body()
            else:
                pl.when(pa < self.owners)(body)

        def unless_owner(self, body):
            if self.owners < RING:
                pl.when(pa >= self.owners)(body)

        def arrived(self, sem, region):
            remote(region, region, self.send.at[0], sem, partner).wait_recv()

        def left(self, which, tiles):
            region = gsum_ref.at[pl.ds(0, tiles)]
            remote(region, region, self.send.at[which], self.recv.at[0], partner).wait_send()

        def pair_sum(self, at, count):
            own = g32[pl.ds(mine + self.at + at, count)]
            return own + self.rc[pl.ds(at, count)].astype(F32)

        def core_start(self):
            remote(g16.at[pl.ds(theirs + self.at, self.count)], self.rc, self.send.at[0],
                   self.recv.at[0], partner).start()

        def scatter(self):
            self.arrived(self.recv.at[0], self.rc)
            self.s16[...] = self.pair_sum(0, self.count).astype(BF16)
            for dx in ORDER:
                px = (x + dx) % NX

                def body(i, carry):
                    p = (pa + RING // 2 + i) % RING

                    def start():
                        remote(self.s16.at[pl.ds((px * self.owners + p) * self.t, self.t)],
                               self.r1.at[(NX - dx) % NX * RING + pa], self.send.at[0],
                               self.recv.at[1], on_plane(px, p)).start()

                    if dx == 0:
                        pl.when((p < self.owners) & (p != pa))(start)
                    elif self.owners < RING:
                        pl.when(p < self.owners)(start)
                    else:
                        start()
                    return carry

                lax.fori_loop(0, RING, body, 0)

        def swap(self):
            def body():
                t = self.t
                self.arrived(self.recv.at[1], self.r1.at[pl.ds(1, NX * RING - 1)])
                self.r1[pa] = jnp.zeros((t, 16, C1), BF16)
                total = self.pair_sum((x * self.owners + pa) * t, t)
                for s in range(NX * RING):
                    total = total + self.r1[s].astype(F32)
                self.e[0] = total.astype(BF16)

                def start(s, carry):
                    remote(self.e.at[0], self.e.at[s], self.send.at[0], self.recv.at[2],
                           on_b((pb + s) % RING)).start()
                    return carry

                lax.fori_loop(1, RING, start, 0)

            self.when_owner(body)

        def region(self, px, p, owners):
            return gsum_ref.at[pl.ds(mine + self.at + px * self.group + p * self.t, owners * self.t)]

        def gather(self):
            def body():
                self.arrived(self.recv.at[2], self.e.at[pl.ds(1, RING - 1)])
                total = self.e[pb % RING].astype(F32)
                for p in range(1, RING):
                    total = total + self.e[(pb - p + RING) % RING].astype(F32)
                own = self.region(x, pa, 1)
                own[...] = total.astype(BF16)
                for dx in ORDER:

                    def start(i, carry):
                        p = (pa + RING // 2 + i) % RING

                        def go():
                            remote(own, own, self.send.at[1], self.late.at[(NX - dx) % NX],
                                   on_plane((x + dx) % NX, p)).start()

                        if dx == 0:
                            pl.when(p != pa)(go)
                        else:
                            go()
                        return carry

                    lax.fori_loop(0, RING, start, 0)

            self.when_owner(body)

        def pass_on(self, g):
            px = (x + g) % NX
            whole = self.region(px, 0, self.owners)
            if g == 0:
                self.when_owner(
                    lambda: self.arrived(self.late.at[0], self.region(px, 0, self.owners - 1))
                )
                self.unless_owner(lambda: self.arrived(self.late.at[0], whole))
            else:
                self.arrived(self.late.at[g], whole)
            remote(whole, whole, self.send.at[1], self.recv.at[3], partner).start()

        def finish(self):
            self.arrived(self.recv.at[3], gsum_ref.at[pl.ds(theirs + self.at, self.count)])
            t, others = self.t, NX * RING - 1

            def owner():
                self.left(0, self.count + (NX * self.owners - 1 + RING - 1) * t)
                self.left(1, self.count + others * t)

            def rest():
                self.left(0, self.count + NX * self.owners * t)
                self.left(1, self.count)

            self.when_owner(owner)
            self.unless_owner(rest)

    down, sub = [Part(i) for i in range(2)]

    grad_down = lax.dot_general(
        kids_ref[...], seeded, (((0,), (0,)), ((), ())), preferred_element_type=F32
    )
    put(SUB, grad_down[:, :C1])
    put(HALF + SUB, grad_down[:, C1:])
    down.core_start()

    slope = sig * (1.0 + preact * (1.0 - sig))
    pre_grad = (hidden_grad * slope * mask).astype(BF16).astype(F32)
    stage_halo(1, pre_grad)
    send_halo(1)
    turned = pre_grad.T.astype(BF16)

    def put_sub(k):
        block = jnp.dot(
            turned, cols_ref[:, k * C1 : (k + 1) * C1], preferred_element_type=F32
        ).T
        if k < 13:
            put(8 * k, block)
        elif k == 13:
            put(8 * k, block[:64])
            put(HALF, block[64:])
        else:
            put(HALF + 8 * k - 108, block)

    for k in range(20):
        put_sub(k)
    down.scatter()
    for k in range(20, 27):
        put_sub(k)
    if SUB > 108:
        for h in range(2):
            put(h * HALF + 108, jnp.zeros(((SUB - 108) * 16, C1), F32))
    sub.core_start()
    center(pre_grad)
    output = jnp.dot(kids_ref[...], wdown_ref[...], preferred_element_type=F32)
    out_ref[...] = (output * coarse).astype(BF16)
    sub.scatter()

    whole_halo(1).wait_recv()
    columns(1)
    gfeat = lax.dot_general(
        cols_ref[...], wflip_ref[...], (((1,), (1,)), ((), ())), preferred_element_type=F32
    )
    gfeat_ref[...] = (gfeat * mask_ref[...]).astype(BF16)

    down.swap()
    sub.swap()
    down.gather()
    sub.gather()
    for part in (down, sub):
        for g in reversed(ORDER):
            part.pass_on(g)
    down.finish()
    sub.finish()
    for which in range(2):
        whole_halo(which).wait_send()


def finish_kernel(
    scale, sums, output_in, gfeat_in, output, gfeat, gsub, gdown,
    sums_ref, output_ref, gfeat_ref, sub_ref, down_ref, in_sem, out_sem,
):
    cuts = ((0, 54), (54, 108), (SUB, HALF))
    loads = {}
    for h in range(2):
        for i, (low, high) in enumerate(cuts):
            region = pl.ds(h * HALF + low, high - low)
            loads[h, i] = pltpu.make_async_copy(sums.at[region], sums_ref.at[region], in_sem.at[h, i])
    for piece in ((0, 0), (0, 1), (1, 0), (1, 1), (0, 2), (1, 2)):
        loads[piece].start()
    small = [
        pltpu.make_async_copy(output_in, output_ref, out_sem.at[0]),
        pltpu.make_async_copy(gfeat_in, gfeat_ref, out_sem.at[1]),
    ]
    for load in small:
        load.start()
    copies = []

    def widened(h, i):
        low, high = cuts[i]
        return (sums_ref[h * HALF + low : h * HALF + high].astype(F32) * scale).reshape(-1, C1)

    def store(src, dst):
        copies.append(pltpu.make_async_copy(src, dst, out_sem.at[2 + len(copies)]))
        copies[-1].start()

    for h in range(2):
        for i in range(2):
            loads[h, i].wait()
            rows = pl.ds((h * 108 + cuts[i][0]) * 16, 54 * 16)
            sub_ref[rows] = widened(h, i)
            store(sub_ref.at[rows], gsub.at[rows])
    for h in range(2):
        loads[h, 2].wait()
        down_ref[:, h * C1 : (h + 1) * C1] = widened(h, 2)
    for r in range(2):
        rows = pl.ds(r * 512, 512)
        store(down_ref.at[rows], gdown.at[rows])
    for load in small:
        load.wait()
    store(output_ref, output)
    store(gfeat_ref, gfeat)
    for copy in copies:
        copy.wait()


def local(features, occupancy, neighbours, weight_sub, weight_down, cotangent):
    def tiles(*shape):
        return pltpu.VMEM(shape + (16, C1), BF16)

    vmem, any_space = pl.BlockSpec(memory_space=pltpu.VMEM), pl.BlockSpec(memory_space=pl.ANY)
    dma = pltpu.SemaphoreType.DMA
    part_scratch = []
    for _, owners, t in PARTS:
        count = NX * owners * t
        part_scratch += [
            tiles(count), tiles(count), tiles(NX * RING, t), tiles(RING, t),
            dma((2,)), dma((4,)), dma((NX,)),
        ]
    output, grad_features, sums = pl.pallas_call(
        kernel,
        out_shape=(
            jax.ShapeDtypeStruct((64, C2), BF16),
            jax.ShapeDtypeStruct((V, C1), BF16),
            jax.ShapeDtypeStruct((2 * HALF, 16, C1), BF16),
        ),
        in_specs=[any_space] * 6,
        out_specs=(vmem, vmem, vmem),
        scratch_shapes=[
            pltpu.SMEM((1, 27), jnp.int32),
            pltpu.VMEM((V, C1), BF16),
            pltpu.VMEM((1, V), jnp.int32),
            pltpu.VMEM((27 * C1, C1), BF16),
            pltpu.VMEM((8 * C1, C2), BF16),
            pltpu.VMEM((64, C2), BF16),
            pltpu.VMEM((V, C1), F32),
            pltpu.VMEM((V, C1), F32),
            pltpu.VMEM((3, 10, 10, 8, C1), F32),
            pltpu.VMEM((V, 27 * C1), BF16),
            pltpu.VMEM((C1, 27 * C1), BF16),
            pltpu.VMEM((64, 8 * C1), BF16),
            tiles(2, 20), tiles(2, 20),
            pltpu.VMEM((2 * HALF, 16, C1), F32),
            tiles(2 * HALF),
            dma((6,)), dma((2,)), dma((2,)),
        ] + part_scratch,
        compiler_params=pltpu.CompilerParams(
            collective_id=0, has_side_effects=True, vmem_limit_bytes=60 * 1024 * 1024
        ),
    )(
        neighbours.reshape(1, 27),
        features.reshape(V, C1),
        occupancy.reshape(1, V),
        weight_sub.reshape(27 * C1, C1),
        weight_down.reshape(8 * C1, C2),
        cotangent.reshape(64, C2),
    )
    scale = 1.0 / math.sqrt(lax.axis_size("gx") * lax.axis_size("gy") * V)
    output, grad_features, grad_sub, grad_down = pl.pallas_call(
        functools.partial(finish_kernel, scale),
        out_shape=(
            jax.ShapeDtypeStruct((64, C2), BF16),
            jax.ShapeDtypeStruct((V, C1), BF16),
            jax.ShapeDtypeStruct((27 * C1, C1), F32),
            jax.ShapeDtypeStruct((8 * C1, C2), F32),
        ),
        in_specs=[any_space] * 3,
        out_specs=(any_space,) * 4,
        scratch_shapes=[
            tiles(2 * HALF), pltpu.VMEM((64, C2), BF16), pltpu.VMEM((V, C1), BF16),
            pltpu.VMEM((27 * C1, C1), F32), pltpu.VMEM((8 * C1, C2), F32), dma((2, 3)), dma((10,)),
        ],
        compiler_params=pltpu.CompilerParams(vmem_limit_bytes=60 * 1024 * 1024),
    )(sums, output, grad_features)
    return (
        output.reshape(1, 1, 1, 64, C2),
        grad_features.reshape(1, 1, 1, V, C1),
        grad_sub.reshape(27, C1, C1),
        grad_down.reshape(8, C1, C2),
    )


def solution(mesh):
    return jax.shard_map(
        local,
        mesh=mesh,
        in_specs=(
            P("gx", "gy", None, None, None),
            P("gx", "gy", None, None),
            P("gx", "gy", None, None),
            P(),
            P(),
            P("gx", "gy", None, None, None),
        ),
        out_specs=(P("gx", "gy", None, None, None), P("gx", "gy", None, None, None), P(), P()),
        check_vma=False,
    )
```

```python
import functools
import math

import jax
import jax.numpy as jnp
from jax import lax
from jax.experimental import pallas as pl
from jax.experimental.pallas import tpu as pltpu
from jax.sharding import PartitionSpec as P

MESH = pl.DeviceIdType.MESH
C1 = 128
C2 = 256
V = 512
X_LO, X_HI, RING = 2, 2, 8
NX = X_LO * X_HI

SUB_OWNERS = RING - 1
SUB_T = -(-108 // (2 * NX * SUB_OWNERS))
SUB_PART = NX * SUB_OWNERS * SUB_T
SUB = 2 * SUB_PART
HALF = SUB + 64
ORDER = (2, 1, 3, 0) if NX == 4 else (1, 0)
PARTS = (
    (SUB, RING, 64 // (NX * RING)),
    (0, SUB_OWNERS, SUB_T),
    (SUB_PART, SUB_OWNERS, SUB_T),
)


FACES = ((1, 0), (-1, 0), (0, 1), (0, -1))
EDGES = ((1, 1), (1, -1), (-1, 1), (-1, -1))

F32 = jnp.float32
BF16 = jnp.bfloat16


def field_slabs(source, minus, zero, plus):
    place = lax.broadcasted_iota(jnp.int32, (1, 8, C1), 1)
    below = jnp.where(place == 0, minus, zero)
    above = jnp.where(place == 7, plus, zero)
    return (
        pltpu.roll(source, 1, axis=1) * below,
        source * zero,
        pltpu.roll(source, 7, axis=1) * above,
    )


def kernel(
    near_in, feat_in, occ_in, wsub_in, wdown_in, cot_in,
    out_ref, gfeat_ref, gsum_ref,
    near_ref, feat_ref, occ_ref, wsub_ref, wdown_ref, cot_ref,
    mask_ref, shuf_ref, field_ref, cols_ref, wflip_ref, kids_ref,
    shalo, rhalo, g32, g16, in_sem, hs_sem, hr_sem, *part_refs,
):
    loads = [
        pltpu.make_async_copy(src, dst, in_sem.at[i])
        for i, (src, dst) in enumerate(
            (
                (occ_in, occ_ref), (feat_in, feat_ref), (near_in, near_ref),
                (wdown_in, wdown_ref), (cot_in, cot_ref), (wsub_in, wsub_ref),
            )
        )
    ]
    gx, gy = lax.axis_index("gx"), lax.axis_index("gy")
    core = gx % 2
    y = (gx // 2) % RING
    x = (gy % X_HI) * X_LO + gx // (2 * RING)
    z = gy // X_HI

    def device(px, py, pz, pc):
        return ((px % X_LO) * (2 * RING) + py * 2 + pc, pz * X_HI + px // X_LO)

    pa = jnp.where(core == 0, y, z)
    pb = jnp.where(core == 0, z, y)

    def on_plane(px, p):
        return device(px, jnp.where(core == 0, p, y), jnp.where(core == 0, z, p), core)

    def on_b(p):
        return device(x, jnp.where(core == 0, y, p), jnp.where(core == 0, p, z), core)

    partner = device(x, y, z, 1 - core)
    tiles_x, tiles_y = 2 * RING * X_LO, RING * X_HI

    def tile_at(dx, dy):
        return ((gx + dx + tiles_x) % tiles_x, (gy + dy + tiles_y) % tiles_y)

    barrier = pltpu.get_barrier_semaphore()

    def greet(target):
        pl.semaphore_signal(barrier, inc=1, device_id=target, device_id_type=MESH)

    for dx, dy in FACES + EDGES:
        greet(tile_at(dx, dy))
    for load in loads:
        load.start()
    greet(partner)

    def greet_plane(i, carry):
        greet(on_plane((x + i // RING) % NX, (pa + i) % RING))
        return carry

    lax.fori_loop(1, NX * RING, greet_plane, 0)

    def greet_ring(s, carry):
        greet(on_b((pb + s) % RING))
        return carry

    lax.fori_loop(1, RING, greet_ring, 0)

    def remote(src, dst, send, recv, target):
        return pltpu.make_async_remote_copy(
            src_ref=src, dst_ref=dst, send_sem=send, recv_sem=recv,
            device_id=target, device_id_type=MESH,
        )

    def send_halo(which):
        for d, (dx, dy) in enumerate(FACES):
            region = pl.ds(4 * d, 4)
            remote(shalo.at[which, region], rhalo.at[which, region], hs_sem.at[which],
                   hr_sem.at[which], tile_at(dx, dy)).start()
        for d, (dx, dy) in enumerate(EDGES):
            region = pl.ds(16 + d, 1)
            remote(shalo.at[which, region], rhalo.at[which, region], hs_sem.at[which],
                   hr_sem.at[which], tile_at(dx, dy)).start()

    def whole_halo(which):
        return remote(shalo.at[which], rhalo.at[which], hs_sem.at[which], hr_sem.at[which], partner)

    def stage_halo(which, value):
        cells = value.reshape(8, 8, 8, C1)
        side = {1: 7, -1: 0}
        for d, (dx, dy) in enumerate(FACES):
            face = cells[side[dx]] if dx else cells[:, side[dy]]
            shalo[which, 4 * d : 4 * d + 4] = face.reshape(4, 16, C1).astype(BF16)
        for d, (dx, dy) in enumerate(EDGES):
            edge = cells[side[dx], side[dy]]
            shalo[which, 16 + d] = jnp.concatenate([edge, edge], axis=0).astype(BF16)

    def named(dx, dy, d0, d1):
        return [
            jnp.where(near_ref[0, 9 * (d0 + 1) + 3 * (d1 + 1) + l] == 3 * (dx + 1) + dy + 1, 1.0, 0.0)
            for l in range(3)
        ]

    def center(value):
        slabs = field_slabs(value.reshape(64, 8, C1), F32(0.0), F32(1.0), F32(0.0))
        for l in range(3):
            field_ref[l, 1:9, 1:9] = slabs[l].reshape(8, 8, 8, C1)

    def columns(which):
        corner = {}

        def add_corner(cx, cy, slabs):
            for l in range(3):
                old = corner.get((cx, cy, l))
                corner[cx, cy, l] = slabs[l] if old is None else old + slabs[l]

        place = {1: 9, -1: 0}
        near_row = {1: 0, -1: 7}
        for dx, dy in FACES:
            slot = FACES.index((-dx, -dy))
            face = rhalo[which, 4 * slot : 4 * slot + 4].astype(F32).reshape(8, 8, C1)
            slabs = field_slabs(face, *named(dx, dy, dx, dy))
            for l in range(3):
                if dx:
                    field_ref[l, place[dx], 1:9] = slabs[l]
                else:
                    for r in range(8):
                        field_ref[l, 1 + r, place[dy]] = slabs[l][r]
            for side in (1, -1):
                row = near_row[side]
                d0, d1 = (dx, side) if dx else (side, dy)
                add_corner(
                    place[d0], place[d1],
                    field_slabs(face[row : row + 1], *named(dx, dy, d0, d1)),
                )
        for dx, dy in EDGES:
            slot = EDGES.index((-dx, -dy))
            edge = rhalo[which, 16 + slot].astype(F32)[0:8].reshape(1, 8, C1)
            add_corner(place[dx], place[dy], field_slabs(edge, *named(dx, dy, dx, dy)))
        for (cx, cy, l), slab in corner.items():
            field_ref[l, cx, cy] = slab[0]
        for i in range(3):
            for j in range(3):
                for l in range(3):
                    k = 9 * i + 3 * j + l
                    window = field_ref[l, i : i + 8, j : j + 8]
                    cols_ref[:, k * C1 : (k + 1) * C1] = window.reshape(V, C1).astype(BF16)

    def split_children(value):
        cells = value.reshape(8, 4, 2, 8, C1)
        for ey in range(2):
            shuf_ref[ey * 256 : (ey + 1) * 256] = cells[:, :, ey].reshape(256, C1)
        children = [None] * 8
        for ey in range(2):
            for ez in range(2):
                half = shuf_ref[pl.ds(ey * 256 + ez, 128, stride=2), :].reshape(4, 2, 16, C1)
                for ex in range(2):
                    children[4 * ex + 2 * ey + ez] = half[:, ex].reshape(64, C1)
        return children

    def join_children(children):
        for ey in range(2):
            for ez in range(2):
                pair = [children[4 * ex + 2 * ey + ez].reshape(4, 1, 16, C1) for ex in range(2)]
                shuf_ref[pl.ds(ey * 256 + ez, 128, stride=2), :] = jnp.concatenate(
                    pair, axis=1
                ).reshape(128, C1)
        sides = [shuf_ref[e * 256 : (e + 1) * 256].reshape(8, 4, 1, 8, C1) for e in range(2)]
        return jnp.concatenate(sides, axis=2).reshape(V, C1)

    loads[0].wait()
    for r in range(4):
        line = occ_ref[0:1, r * 128 : (r + 1) * 128].astype(F32)
        mask_ref[r * 128 : (r + 1) * 128] = jnp.broadcast_to(line, (128, 128)).T
    loads[1].wait()
    masked = feat_ref[...].astype(F32) * mask_ref[...]
    stage_halo(0, masked)
    pl.semaphore_wait(barrier, 9 + NX * RING - 1 + RING - 1)
    send_halo(0)

    center(masked)
    for load in loads[2:]:
        load.wait()
    for k in range(27):
        wflip_ref[:, k * C1 : (k + 1) * C1] = wsub_ref[(26 - k) * C1 : (27 - k) * C1]
    coarse = None
    for child in split_children(mask_ref[...]):
        coarse = child if coarse is None else jnp.maximum(coarse, child)
    coarse = jnp.concatenate([coarse, coarse], axis=1)
    seeded = (cot_ref[...].astype(F32) * coarse).astype(BF16)
    spread = lax.dot_general(
        seeded, wdown_ref[...], (((1,), (1,)), ((), ())), preferred_element_type=F32
    )
    hidden_grad = join_children([spread[:, r * C1 : (r + 1) * C1] for r in range(8)])

    whole_halo(0).wait_recv()
    columns(0)
    preact = jnp.dot(cols_ref[...], wsub_ref[...], preferred_element_type=F32)
    sig = jax.nn.sigmoid(preact)
    mask = mask_ref[...]
    hidden = (preact * sig * mask).astype(BF16).astype(F32)
    for r, child in enumerate(split_children(hidden)):
        kids_ref[:, r * C1 : (r + 1) * C1] = child.astype(BF16)

    mine, theirs = core * HALF, (1 - core) * HALF

    def put(tile, value):
        value = value.reshape(value.shape[0] // 16, 16, C1)
        g32[tile : tile + value.shape[0]] = value
        g16[tile : tile + value.shape[0]] = value.astype(BF16)

    class Part:
        def __init__(self, index):
            self.at, self.owners, self.t = PARTS[index]
            self.group = self.owners * self.t
            self.count = NX * self.group
            (self.rc, self.s16, self.r1, self.e,
             self.send, self.recv, self.late) = part_refs[7 * index : 7 * index + 7]

        def when_owner(self, body):
            if self.owners == RING:
                body()
            else:
                pl.when(pa < self.owners)(body)

        def unless_owner(self, body):
            if self.owners < RING:
                pl.when(pa >= self.owners)(body)

        def arrived(self, sem, region):
            remote(region, region, self.send.at[0], sem, partner).wait_recv()

        def left(self, which, tiles):
            region = gsum_ref.at[pl.ds(0, tiles)]
            remote(region, region, self.send.at[which], self.recv.at[0], partner).wait_send()

        def pair_sum(self, at, count):
            own = g32[pl.ds(mine + self.at + at, count)]
            return own + self.rc[pl.ds(at, count)].astype(F32)

        def core_start(self):
            remote(g16.at[pl.ds(theirs + self.at, self.count)], self.rc, self.send.at[0],
                   self.recv.at[0], partner).start()

        def scatter(self):
            self.arrived(self.recv.at[0], self.rc)
            self.s16[...] = self.pair_sum(0, self.count).astype(BF16)
            for dx in ORDER:
                px = (x + dx) % NX

                def body(i, carry):
                    p = (pa + RING // 2 + i) % RING

                    def start():
                        remote(self.s16.at[pl.ds((px * self.owners + p) * self.t, self.t)],
                               self.r1.at[(NX - dx) % NX * RING + pa], self.send.at[0],
                               self.recv.at[1], on_plane(px, p)).start()

                    if dx == 0:
                        pl.when((p < self.owners) & (p != pa))(start)
                    elif self.owners < RING:
                        pl.when(p < self.owners)(start)
                    else:
                        start()
                    return carry

                lax.fori_loop(0, RING, body, 0)

        def swap(self):
            def body():
                t = self.t
                self.arrived(self.recv.at[1], self.r1.at[pl.ds(1, NX * RING - 1)])
                self.r1[pa] = jnp.zeros((t, 16, C1), BF16)
                total = self.pair_sum((x * self.owners + pa) * t, t)
                for s in range(NX * RING):
                    total = total + self.r1[s].astype(F32)
                self.e[0] = total.astype(BF16)

                def start(s, carry):
                    remote(self.e.at[0], self.e.at[s], self.send.at[0], self.recv.at[2],
                           on_b((pb + s) % RING)).start()
                    return carry

                lax.fori_loop(1, RING, start, 0)

            self.when_owner(body)

        def region(self, px, p, owners):
            return gsum_ref.at[pl.ds(mine + self.at + px * self.group + p * self.t, owners * self.t)]

        def gather(self):
            def body():
                self.arrived(self.recv.at[2], self.e.at[pl.ds(1, RING - 1)])
                total = self.e[pb % RING].astype(F32)
                for p in range(1, RING):
                    total = total + self.e[(pb - p + RING) % RING].astype(F32)
                own = self.region(x, pa, 1)
                own[...] = total.astype(BF16)
                for dx in ORDER:

                    def start(i, carry):
                        p = (pa + RING // 2 + i) % RING

                        def go():
                            remote(own, own, self.send.at[1], self.late.at[(NX - dx) % NX],
                                   on_plane((x + dx) % NX, p)).start()

                        if dx == 0:
                            pl.when(p != pa)(go)
                        else:
                            go()
                        return carry

                    lax.fori_loop(0, RING, start, 0)

            self.when_owner(body)

        def pass_on(self, g):
            px = (x + g) % NX
            whole = self.region(px, 0, self.owners)
            if g == 0:
                self.when_owner(
                    lambda: self.arrived(self.late.at[0], self.region(px, 0, self.owners - 1))
                )
                self.unless_owner(lambda: self.arrived(self.late.at[0], whole))
            else:
                self.arrived(self.late.at[g], whole)
            remote(whole, whole, self.send.at[1], self.recv.at[3], partner).start()

        def finish(self):
            self.arrived(self.recv.at[3], gsum_ref.at[pl.ds(theirs + self.at, self.count)])
            t, others = self.t, NX * RING - 1

            def owner():
                self.left(0, self.count + (NX * self.owners - 1 + RING - 1) * t)
                self.left(1, self.count + others * t)

            def rest():
                self.left(0, self.count + NX * self.owners * t)
                self.left(1, self.count)

            self.when_owner(owner)
            self.unless_owner(rest)

    down, sub1, sub2 = [Part(i) for i in range(3)]

    grad_down = lax.dot_general(
        kids_ref[...], seeded, (((0,), (0,)), ((), ())), preferred_element_type=F32
    )
    put(SUB, grad_down[:, :C1])
    put(HALF + SUB, grad_down[:, C1:])
    down.core_start()

    slope = sig * (1.0 + preact * (1.0 - sig))
    pre_grad = (hidden_grad * slope * mask).astype(BF16).astype(F32)
    stage_halo(1, pre_grad)
    send_halo(1)
    turned = pre_grad.T.astype(BF16)

    def put_sub(low, high):
        blocks = jnp.dot(
            turned, cols_ref[:, low * C1 : high * C1], preferred_element_type=F32
        )
        for k in range(low, high):
            block = blocks[:, (k - low) * C1 : (k - low + 1) * C1].T
            if k < 13:
                put(8 * k, block)
            elif k == 13:
                put(8 * k, block[:64])
                put(HALF, block[64:])
            else:
                put(HALF + 8 * k - 108, block)

    first = -(-SUB_PART // 8)
    second = -(-(108 + SUB_PART) // 8)
    put_sub(0, first)
    put_sub(13, second)
    sub1.core_start()
    down.scatter()
    put_sub(first, 13)
    put_sub(second, 27)
    if SUB > 108:
        for h in range(2):
            put(h * HALF + 108, jnp.zeros(((SUB - 108) * 16, C1), F32))
    sub2.core_start()
    sub1.scatter()
    center(pre_grad)
    sub2.scatter()

    whole_halo(1).wait_recv()
    columns(1)
    gfeat = lax.dot_general(
        cols_ref[...], wflip_ref[...], (((1,), (1,)), ((), ())), preferred_element_type=F32
    )
    gfeat_ref[...] = (gfeat * mask_ref[...]).astype(BF16)
    output = jnp.dot(kids_ref[...], wdown_ref[...], preferred_element_type=F32)
    out_ref[...] = (output * coarse).astype(BF16)

    parts = (down, sub1, sub2)
    for part in parts:
        part.swap()
    for part in parts:
        part.gather()
    for part in parts:
        for g in reversed(ORDER):
            part.pass_on(g)
    for part in parts:
        part.finish()
    for which in range(2):
        whole_halo(which).wait_send()


def finish_kernel(
    scale, sums_ref, output_ref, gfeat_ref, output, gfeat, gsub, gdown, sub_ref, down_ref, sem
):
    copies = []

    def store(src, dst):
        copies.append(pltpu.make_async_copy(src, dst, sem.at[len(copies)]))
        copies[-1].start()

    def widened(low, high):
        return (sums_ref[low:high].astype(F32) * scale).reshape(-1, C1)

    for h in range(2):
        for i in range(3):
            rows = pl.ds((h * 108 + i * 36) * 16, 36 * 16)
            sub_ref[rows] = widened(h * HALF + i * 36, h * HALF + i * 36 + 36)
            store(sub_ref.at[rows], gsub.at[rows])
    for r in range(2):
        rows = pl.ds(r * 512, 512)
        for h in range(2):
            low = h * HALF + SUB + r * 32
            down_ref[rows, h * C1 : (h + 1) * C1] = widened(low, low + 32)
        store(down_ref.at[rows], gdown.at[rows])
    store(output_ref, output)
    store(gfeat_ref, gfeat)
    for copy in copies:
        copy.wait()


def local(features, occupancy, neighbours, weight_sub, weight_down, cotangent):
    def tiles(*shape):
        return pltpu.VMEM(shape + (16, C1), BF16)

    vmem, any_space = pl.BlockSpec(memory_space=pltpu.VMEM), pl.BlockSpec(memory_space=pl.ANY)
    dma = pltpu.SemaphoreType.DMA
    part_scratch = []
    for _, owners, t in PARTS:
        count = NX * owners * t
        part_scratch += [
            tiles(count), tiles(count), tiles(NX * RING, t), tiles(RING, t),
            dma((2,)), dma((4,)), dma((NX,)),
        ]
    output, grad_features, sums = pl.pallas_call(
        kernel,
        out_shape=(
            pltpu.VMEM((64, C2), BF16), pltpu.VMEM((V, C1), BF16), tiles(2 * HALF),
        ),
        in_specs=[any_space] * 6,
        out_specs=(vmem,) * 3,
        scratch_shapes=[
            pltpu.SMEM((1, 27), jnp.int32),
            pltpu.VMEM((V, C1), BF16),
            pltpu.VMEM((1, V), jnp.int32),
            pltpu.VMEM((27 * C1, C1), BF16),
            pltpu.VMEM((8 * C1, C2), BF16),
            pltpu.VMEM((64, C2), BF16),
            pltpu.VMEM((V, C1), F32),
            pltpu.VMEM((V, C1), F32),
            pltpu.VMEM((3, 10, 10, 8, C1), F32),
            pltpu.VMEM((V, 27 * C1), BF16),
            pltpu.VMEM((C1, 27 * C1), BF16),
            pltpu.VMEM((64, 8 * C1), BF16),
            tiles(2, 20), tiles(2, 20),
            pltpu.VMEM((2 * HALF, 16, C1), F32),
            tiles(2 * HALF),
            dma((6,)), dma((2,)), dma((2,)),
        ] + part_scratch,
        compiler_params=pltpu.CompilerParams(
            collective_id=0, has_side_effects=True, vmem_limit_bytes=40 * 1024 * 1024
        ),
    )(
        *(
            pltpu.with_memory_space_constraint(arg, pltpu.HBM)
            for arg in (
                neighbours.reshape(1, 27),
                features.reshape(V, C1),
                occupancy.reshape(1, V),
                weight_sub.reshape(27 * C1, C1),
                weight_down.reshape(8 * C1, C2),
                cotangent.reshape(64, C2),
            )
        )
    )
    scale = 1.0 / math.sqrt(lax.axis_size("gx") * lax.axis_size("gy") * V)
    output, grad_features, grad_sub, grad_down = pl.pallas_call(
        functools.partial(finish_kernel, scale),
        out_shape=(
            jax.ShapeDtypeStruct((64, C2), BF16),
            jax.ShapeDtypeStruct((V, C1), BF16),
            jax.ShapeDtypeStruct((27 * C1, C1), F32),
            jax.ShapeDtypeStruct((8 * C1, C2), F32),
        ),
        in_specs=[vmem] * 3,
        out_specs=(any_space,) * 4,
        scratch_shapes=[
            pltpu.VMEM((27 * C1, C1), F32), pltpu.VMEM((8 * C1, C2), F32), dma((10,)),
        ],
        compiler_params=pltpu.CompilerParams(vmem_limit_bytes=16 * 1024 * 1024),
    )(sums, output, grad_features)
    return (
        output.reshape(1, 1, 1, 64, C2),
        grad_features.reshape(1, 1, 1, V, C1),
        grad_sub.reshape(27, C1, C1),
        grad_down.reshape(8, C1, C2),
    )


def solution(mesh):
    return jax.shard_map(
        local,
        mesh=mesh,
        in_specs=(
            P("gx", "gy", None, None, None),
            P("gx", "gy", None, None),
            P("gx", "gy", None, None),
            P(),
            P(),
            P("gx", "gy", None, None, None),
        ),
        out_specs=(P("gx", "gy", None, None, None), P("gx", "gy", None, None, None), P(), P()),
        check_vma=False,
    )
```

```python
import functools
import math

import jax
import jax.numpy as jnp
from jax import lax
from jax.experimental import pallas as pl
from jax.experimental.pallas import tpu as pltpu
from jax.sharding import PartitionSpec as P

MESH = pl.DeviceIdType.MESH
C1 = 128
C2 = 256
V = 512
X_LO, X_HI, RING = 2, 2, 8
NX = X_LO * X_HI

DOWN_PARTS, SUB_PARTS = 1, 2
SUB_OWNERS = RING - 1
SUB_T = -(-108 // (SUB_PARTS * NX * SUB_OWNERS))
SUB_PART = NX * SUB_OWNERS * SUB_T
SUB = SUB_PARTS * SUB_PART
DOWN_PART = 64 // DOWN_PARTS
HALF = SUB + 64
ORDER = (2, 1, 3, 0) if NX == 4 else (1, 0)
PARTS = [
    (SUB + i * DOWN_PART, RING, DOWN_PART // (NX * RING)) for i in range(DOWN_PARTS)
] + [(i * SUB_PART, SUB_OWNERS, SUB_T) for i in range(SUB_PARTS)]


FACES = ((1, 0), (-1, 0), (0, 1), (0, -1))
EDGES = ((1, 1), (1, -1), (-1, 1), (-1, -1))

F32 = jnp.float32
BF16 = jnp.bfloat16


def field_slabs(source, minus, zero, plus):
    place = lax.broadcasted_iota(jnp.int32, (1, 8, C1), 1)
    below = jnp.where(place == 0, minus, zero)
    above = jnp.where(place == 7, plus, zero)
    return (
        pltpu.roll(source, 1, axis=1) * below,
        source * zero,
        pltpu.roll(source, 7, axis=1) * above,
    )


def kernel(
    near_in, feat_in, occ_in, wsub_in, wdown_in, cot_in,
    out_ref, gfeat_ref, gsum_ref,
    near_ref, feat_ref, occ_ref, wsub_ref, wdown_ref, cot_ref,
    mask_ref, shuf_ref, field_ref, cols_ref, wflip_ref, kids_ref,
    shalo, rhalo, g32, g16, in_sem, hs_sem, hr_sem, *part_refs,
):
    loads = [
        pltpu.make_async_copy(src, dst, in_sem.at[i])
        for i, (src, dst) in enumerate(
            (
                (occ_in, occ_ref), (feat_in, feat_ref), (near_in, near_ref),
                (wdown_in, wdown_ref), (cot_in, cot_ref), (wsub_in, wsub_ref),
            )
        )
    ]
    gx, gy = lax.axis_index("gx"), lax.axis_index("gy")
    core = gx % 2
    y = (gx // 2) % RING
    x = (gy % X_HI) * X_LO + gx // (2 * RING)
    z = gy // X_HI

    def device(px, py, pz, pc):
        return ((px % X_LO) * (2 * RING) + py * 2 + pc, pz * X_HI + px // X_LO)

    pa = jnp.where(core == 0, y, z)
    pb = jnp.where(core == 0, z, y)

    def on_plane(px, p):
        return device(px, jnp.where(core == 0, p, y), jnp.where(core == 0, z, p), core)

    def on_b(p):
        return device(x, jnp.where(core == 0, y, p), jnp.where(core == 0, p, z), core)

    partner = device(x, y, z, 1 - core)
    tiles_x, tiles_y = 2 * RING * X_LO, RING * X_HI

    def tile_at(dx, dy):
        return ((gx + dx + tiles_x) % tiles_x, (gy + dy + tiles_y) % tiles_y)

    places = [(pa + d) % RING for d in range(RING)]
    barrier = pltpu.get_barrier_semaphore()

    def greet(target):
        pl.semaphore_signal(barrier, inc=1, device_id=target, device_id_type=MESH)

    row = [jnp.where(core == 0, p, y) * 2 + core for p in places]
    column = [jnp.where(core == 0, z, p) * X_HI for p in places]
    x_low = [((x + dx) % NX) % X_LO * (2 * RING) for dx in range(NX)]
    x_high = [((x + dx) % NX) // X_LO for dx in range(NX)]
    plane = [(dx, d) for dx in range(NX) for d in range(RING) if dx or d]
    plane.sort(key=lambda step: -min(step[0], NX - step[0]) - min(step[1], RING - step[1]))

    def greet_plane(steps):
        for dx, d in steps:
            greet((x_low[dx] + row[d], column[d] + x_high[dx]))

    far = len(plane) * 2 // 5
    greet_plane(plane[:far])
    for dx, dy in FACES + EDGES:
        greet(tile_at(dx, dy))
    for d in range(1, RING):
        greet(on_b((pb + d) % RING))
    greet_plane(plane[far:])
    greet(partner)
    for load in loads:
        load.start()

    def remote(src, dst, send, recv, target):
        return pltpu.make_async_remote_copy(
            src_ref=src, dst_ref=dst, send_sem=send, recv_sem=recv,
            device_id=target, device_id_type=MESH,
        )

    def send_halo(which):
        for d, (dx, dy) in enumerate(FACES):
            region = pl.ds(4 * d, 4)
            remote(shalo.at[which, region], rhalo.at[which, region], hs_sem.at[which],
                   hr_sem.at[which], tile_at(dx, dy)).start()
        for d, (dx, dy) in enumerate(EDGES):
            region = pl.ds(16 + d, 1)
            remote(shalo.at[which, region], rhalo.at[which, region], hs_sem.at[which],
                   hr_sem.at[which], tile_at(dx, dy)).start()

    def whole_halo(which):
        return remote(shalo.at[which], rhalo.at[which], hs_sem.at[which], hr_sem.at[which], partner)

    def stage_halo(which, value):
        cells = value.reshape(8, 8, 8, C1)
        side = {1: 7, -1: 0}
        for d, (dx, dy) in enumerate(FACES):
            face = cells[side[dx]] if dx else cells[:, side[dy]]
            shalo[which, 4 * d : 4 * d + 4] = face.reshape(4, 16, C1).astype(BF16)
        for d, (dx, dy) in enumerate(EDGES):
            edge = cells[side[dx], side[dy]]
            shalo[which, 16 + d] = jnp.concatenate([edge, edge], axis=0).astype(BF16)

    def named(dx, dy, d0, d1):
        return [
            jnp.where(near_ref[0, 9 * (d0 + 1) + 3 * (d1 + 1) + l] == 3 * (dx + 1) + dy + 1, 1.0, 0.0)
            for l in range(3)
        ]

    def center(value):
        slabs = field_slabs(value.reshape(64, 8, C1), F32(0.0), F32(1.0), F32(0.0))
        for l in range(3):
            field_ref[l, 1:9, 1:9] = slabs[l].reshape(8, 8, 8, C1)

    def columns(which):
        corner = {}

        def add_corner(cx, cy, slabs):
            for l in range(3):
                old = corner.get((cx, cy, l))
                corner[cx, cy, l] = slabs[l] if old is None else old + slabs[l]

        place = {1: 9, -1: 0}
        near_row = {1: 0, -1: 7}
        for dx, dy in FACES:
            slot = FACES.index((-dx, -dy))
            face = rhalo[which, 4 * slot : 4 * slot + 4].astype(F32).reshape(8, 8, C1)
            slabs = field_slabs(face, *named(dx, dy, dx, dy))
            for l in range(3):
                if dx:
                    field_ref[l, place[dx], 1:9] = slabs[l]
                else:
                    for r in range(8):
                        field_ref[l, 1 + r, place[dy]] = slabs[l][r]
            for side in (1, -1):
                row = near_row[side]
                d0, d1 = (dx, side) if dx else (side, dy)
                add_corner(
                    place[d0], place[d1],
                    field_slabs(face[row : row + 1], *named(dx, dy, d0, d1)),
                )
        for dx, dy in EDGES:
            slot = EDGES.index((-dx, -dy))
            edge = rhalo[which, 16 + slot].astype(F32)[0:8].reshape(1, 8, C1)
            add_corner(place[dx], place[dy], field_slabs(edge, *named(dx, dy, dx, dy)))
        for (cx, cy, l), slab in corner.items():
            field_ref[l, cx, cy] = slab[0]
        for i in range(3):
            for j in range(3):
                for l in range(3):
                    k = 9 * i + 3 * j + l
                    window = field_ref[l, i : i + 8, j : j + 8]
                    cols_ref[:, k * C1 : (k + 1) * C1] = window.reshape(V, C1).astype(BF16)

    def split_children(value):
        cells = value.reshape(8, 4, 2, 8, C1)
        for ey in range(2):
            shuf_ref[ey * 256 : (ey + 1) * 256] = cells[:, :, ey].reshape(256, C1)
        children = [None] * 8
        for ey in range(2):
            for ez in range(2):
                half = shuf_ref[pl.ds(ey * 256 + ez, 128, stride=2), :].reshape(4, 2, 16, C1)
                for ex in range(2):
                    children[4 * ex + 2 * ey + ez] = half[:, ex].reshape(64, C1)
        return children

    def join_children(children):
        for ey in range(2):
            for ez in range(2):
                pair = [children[4 * ex + 2 * ey + ez].reshape(4, 1, 16, C1) for ex in range(2)]
                shuf_ref[pl.ds(ey * 256 + ez, 128, stride=2), :] = jnp.concatenate(
                    pair, axis=1
                ).reshape(128, C1)
        sides = [shuf_ref[e * 256 : (e + 1) * 256].reshape(8, 4, 1, 8, C1) for e in range(2)]
        return jnp.concatenate(sides, axis=2).reshape(V, C1)

    loads[0].wait()
    for r in range(4):
        line = occ_ref[0:1, r * 128 : (r + 1) * 128].astype(F32)
        mask_ref[r * 128 : (r + 1) * 128] = jnp.broadcast_to(line, (128, 128)).T
    loads[1].wait()
    masked = feat_ref[...].astype(F32) * mask_ref[...]
    stage_halo(0, masked)
    pl.semaphore_wait(barrier, 9 + NX * RING - 1 + RING - 1)
    send_halo(0)

    center(masked)
    for load in loads[2:]:
        load.wait()
    for k in range(27):
        wflip_ref[:, k * C1 : (k + 1) * C1] = wsub_ref[(26 - k) * C1 : (27 - k) * C1]
    coarse = None
    for child in split_children(mask_ref[...]):
        coarse = child if coarse is None else jnp.maximum(coarse, child)
    coarse = jnp.concatenate([coarse, coarse], axis=1)
    seeded = (cot_ref[...].astype(F32) * coarse).astype(BF16)
    spread = lax.dot_general(
        seeded, wdown_ref[...], (((1,), (1,)), ((), ())), preferred_element_type=F32
    )
    hidden_grad = join_children([spread[:, r * C1 : (r + 1) * C1] for r in range(8)])

    whole_halo(0).wait_recv()
    columns(0)
    preact = jnp.dot(cols_ref[...], wsub_ref[...], preferred_element_type=F32)
    sig = jax.nn.sigmoid(preact)
    mask = mask_ref[...]
    hidden = (preact * sig * mask).astype(BF16).astype(F32)
    for r, child in enumerate(split_children(hidden)):
        kids_ref[:, r * C1 : (r + 1) * C1] = child.astype(BF16)

    mine, theirs = core * HALF, (1 - core) * HALF

    def put(tile, value):
        value = value.reshape(value.shape[0] // 16, 16, C1)
        g32[tile : tile + value.shape[0]] = value
        g16[tile : tile + value.shape[0]] = value.astype(BF16)

    class Part:
        def __init__(self, index):
            self.at, self.owners, self.t = PARTS[index]
            self.group = self.owners * self.t
            self.count = NX * self.group
            (self.rc, self.s16, self.r1, self.e,
             self.send, self.recv, self.late) = part_refs[7 * index : 7 * index + 7]

        def when_owner(self, body):
            if self.owners == RING:
                body()
            else:
                pl.when(pa < self.owners)(body)

        def unless_owner(self, body):
            if self.owners < RING:
                pl.when(pa >= self.owners)(body)

        def arrived(self, sem, region):
            remote(region, region, self.send.at[0], sem, partner).wait_recv()

        def left(self, which, tiles):
            region = gsum_ref.at[pl.ds(0, tiles)]
            remote(region, region, self.send.at[which], self.recv.at[0], partner).wait_send()

        def pair_sum(self, at, count):
            own = g32[pl.ds(mine + self.at + at, count)]
            return own + self.rc[pl.ds(at, count)].astype(F32)

        def core_start(self):
            remote(g16.at[pl.ds(theirs + self.at, self.count)], self.rc, self.send.at[0],
                   self.recv.at[0], partner).start()

        def scatter(self):
            self.arrived(self.recv.at[0], self.rc)
            self.s16[...] = self.pair_sum(0, self.count).astype(BF16)
            for dx in ORDER:
                px = (x + dx) % NX

                def body(i, carry):
                    p = (pa + RING // 2 + i) % RING

                    def start():
                        remote(self.s16.at[pl.ds((px * self.owners + p) * self.t, self.t)],
                               self.r1.at[(NX - dx) % NX * RING + pa], self.send.at[0],
                               self.recv.at[1], on_plane(px, p)).start()

                    if dx == 0:
                        pl.when((p < self.owners) & (p != pa))(start)
                    elif self.owners < RING:
                        pl.when(p < self.owners)(start)
                    else:
                        start()
                    return carry

                lax.fori_loop(0, RING, body, 0)

        def swap(self):
            def body():
                t = self.t
                self.arrived(self.recv.at[1], self.r1.at[pl.ds(1, NX * RING - 1)])
                self.r1[pa] = jnp.zeros((t, 16, C1), BF16)
                total = self.pair_sum((x * self.owners + pa) * t, t)
                for s in range(NX * RING):
                    total = total + self.r1[s].astype(F32)
                self.e[0] = total.astype(BF16)

                def start(s, carry):
                    remote(self.e.at[0], self.e.at[s], self.send.at[0], self.recv.at[2],
                           on_b((pb + s) % RING)).start()
                    return carry

                lax.fori_loop(1, RING, start, 0)

            self.when_owner(body)

        def region(self, px, p, owners):
            return gsum_ref.at[pl.ds(mine + self.at + px * self.group + p * self.t, owners * self.t)]

        def gather(self):
            def body():
                self.arrived(self.recv.at[2], self.e.at[pl.ds(1, RING - 1)])
                total = self.e[pb % RING].astype(F32)
                for p in range(1, RING):
                    total = total + self.e[(pb - p + RING) % RING].astype(F32)
                own = self.region(x, pa, 1)
                own[...] = total.astype(BF16)
                for dx in ORDER:

                    def start(i, carry):
                        p = (pa + RING // 2 + i) % RING

                        def go():
                            remote(own, own, self.send.at[1], self.late.at[(NX - dx) % NX],
                                   on_plane((x + dx) % NX, p)).start()

                        if dx == 0:
                            pl.when(p != pa)(go)
                        else:
                            go()
                        return carry

                    lax.fori_loop(0, RING, start, 0)

            self.when_owner(body)

        def pass_on(self, g):
            px = (x + g) % NX
            whole = self.region(px, 0, self.owners)
            if g == 0:
                self.when_owner(
                    lambda: self.arrived(self.late.at[0], self.region(px, 0, self.owners - 1))
                )
                self.unless_owner(lambda: self.arrived(self.late.at[0], whole))
            else:
                self.arrived(self.late.at[g], whole)
            remote(whole, whole, self.send.at[1], self.recv.at[3], partner).start()

        def finish(self):
            self.arrived(self.recv.at[3], gsum_ref.at[pl.ds(theirs + self.at, self.count)])
            t, others = self.t, NX * RING - 1

            def owner():
                self.left(0, self.count + (NX * self.owners - 1 + RING - 1) * t)
                self.left(1, self.count + others * t)

            def rest():
                self.left(0, self.count + NX * self.owners * t)
                self.left(1, self.count)

            self.when_owner(owner)
            self.unless_owner(rest)

    parts = [Part(i) for i in range(DOWN_PARTS + SUB_PARTS)]
    split = DOWN_PARTS + SUB_PARTS // 2

    grad_down = lax.dot_general(
        kids_ref[...], seeded, (((0,), (0,)), ((), ())), preferred_element_type=F32
    )
    put(SUB, grad_down[:, :C1])
    put(HALF + SUB, grad_down[:, C1:])
    for part in parts[:DOWN_PARTS]:
        part.core_start()

    slope = sig * (1.0 + preact * (1.0 - sig))
    pre_grad = (hidden_grad * slope * mask).astype(BF16).astype(F32)
    turned = pre_grad.T.astype(BF16)

    def put_sub(low, high):
        blocks = jnp.dot(
            turned, cols_ref[:, low * C1 : high * C1], preferred_element_type=F32
        )
        for k in range(low, high):
            block = blocks[:, (k - low) * C1 : (k - low + 1) * C1].T
            if k < 13:
                put(8 * k, block)
            elif k == 13:
                put(8 * k, block[:64])
                put(HALF, block[64:])
            else:
                put(HALF + 8 * k - 108, block)

    early = SUB_PARTS // 2 * SUB_PART
    first = -(-early // 8)
    second = -(-(108 + early) // 8)
    put_sub(0, first)
    put_sub(13, second)
    for part in parts[DOWN_PARTS:split]:
        part.core_start()
    put_sub(first, 13)
    put_sub(second, 27)
    if SUB > 108:
        for h in range(2):
            put(h * HALF + 108, jnp.zeros(((SUB - 108) * 16, C1), F32))
    for part in parts[split:]:
        part.core_start()
    for part in parts:
        part.scatter()
    stage_halo(1, pre_grad)
    send_halo(1)

    for part in parts:
        part.swap()
    for part in parts:
        part.gather()

    center(pre_grad)
    whole_halo(1).wait_recv()
    columns(1)
    gfeat = lax.dot_general(
        cols_ref[...], wflip_ref[...], (((1,), (1,)), ((), ())), preferred_element_type=F32
    )
    gfeat_ref[...] = (gfeat * mask_ref[...]).astype(BF16)
    output = jnp.dot(kids_ref[...], wdown_ref[...], preferred_element_type=F32)
    out_ref[...] = (output * coarse).astype(BF16)

    for part in parts:
        for g in ORDER:
            part.pass_on(g)
    for part in parts:
        part.finish()
    for which in range(2):
        whole_halo(which).wait_send()


def finish_kernel(
    scale, sums_ref, output_ref, gfeat_ref, output, gfeat, gsub, gdown, sub_ref, down_ref, sem
):
    copies = []

    def store(src, dst):
        copies.append(pltpu.make_async_copy(src, dst, sem.at[len(copies)]))
        copies[-1].start()

    def widened(low, high):
        return (sums_ref[low:high].astype(F32) * scale).reshape(-1, C1)

    for h in range(2):
        for i in range(3):
            rows = pl.ds((h * 108 + i * 36) * 16, 36 * 16)
            sub_ref[rows] = widened(h * HALF + i * 36, h * HALF + i * 36 + 36)
            store(sub_ref.at[rows], gsub.at[rows])
    for r in range(2):
        rows = pl.ds(r * 512, 512)
        for h in range(2):
            low = h * HALF + SUB + r * 32
            down_ref[rows, h * C1 : (h + 1) * C1] = widened(low, low + 32)
        store(down_ref.at[rows], gdown.at[rows])
    store(output_ref, output)
    store(gfeat_ref, gfeat)
    for copy in copies:
        copy.wait()


def local(features, occupancy, neighbours, weight_sub, weight_down, cotangent):
    def tiles(*shape):
        return pltpu.VMEM(shape + (16, C1), BF16)

    vmem, any_space = pl.BlockSpec(memory_space=pltpu.VMEM), pl.BlockSpec(memory_space=pl.ANY)
    dma = pltpu.SemaphoreType.DMA
    part_scratch = []
    for _, owners, t in PARTS:
        count = NX * owners * t
        part_scratch += [
            tiles(count), tiles(count), tiles(NX * RING, t), tiles(RING, t),
            dma((2,)), dma((4,)), dma((NX,)),
        ]
    output, grad_features, sums = pl.pallas_call(
        kernel,
        out_shape=(
            pltpu.VMEM((64, C2), BF16), pltpu.VMEM((V, C1), BF16), tiles(2 * HALF),
        ),
        in_specs=[any_space] * 6,
        out_specs=(vmem,) * 3,
        scratch_shapes=[
            pltpu.SMEM((1, 27), jnp.int32),
            pltpu.VMEM((V, C1), BF16),
            pltpu.VMEM((1, V), jnp.int32),
            pltpu.VMEM((27 * C1, C1), BF16),
            pltpu.VMEM((8 * C1, C2), BF16),
            pltpu.VMEM((64, C2), BF16),
            pltpu.VMEM((V, C1), F32),
            pltpu.VMEM((V, C1), F32),
            pltpu.VMEM((3, 10, 10, 8, C1), F32),
            pltpu.VMEM((V, 27 * C1), BF16),
            pltpu.VMEM((C1, 27 * C1), BF16),
            pltpu.VMEM((64, 8 * C1), BF16),
            tiles(2, 20), tiles(2, 20),
            pltpu.VMEM((2 * HALF, 16, C1), F32),
            tiles(2 * HALF),
            dma((6,)), dma((2,)), dma((2,)),
        ] + part_scratch,
        compiler_params=pltpu.CompilerParams(
            collective_id=0, has_side_effects=True, vmem_limit_bytes=40 * 1024 * 1024
        ),
    )(
        *(
            pltpu.with_memory_space_constraint(arg, pltpu.HBM)
            for arg in (
                neighbours.reshape(1, 27),
                features.reshape(V, C1),
                occupancy.reshape(1, V),
                weight_sub.reshape(27 * C1, C1),
                weight_down.reshape(8 * C1, C2),
                cotangent.reshape(64, C2),
            )
        )
    )
    scale = 1.0 / math.sqrt(lax.axis_size("gx") * lax.axis_size("gy") * V)
    output, grad_features, grad_sub, grad_down = pl.pallas_call(
        functools.partial(finish_kernel, scale),
        out_shape=(
            jax.ShapeDtypeStruct((64, C2), BF16),
            jax.ShapeDtypeStruct((V, C1), BF16),
            jax.ShapeDtypeStruct((27 * C1, C1), F32),
            jax.ShapeDtypeStruct((8 * C1, C2), F32),
        ),
        in_specs=[vmem] * 3,
        out_specs=(any_space,) * 4,
        scratch_shapes=[
            pltpu.VMEM((27 * C1, C1), F32), pltpu.VMEM((8 * C1, C2), F32), dma((10,)),
        ],
        compiler_params=pltpu.CompilerParams(vmem_limit_bytes=16 * 1024 * 1024),
    )(sums, output, grad_features)
    return (
        output.reshape(1, 1, 1, 64, C2),
        grad_features.reshape(1, 1, 1, V, C1),
        grad_sub.reshape(27, C1, C1),
        grad_down.reshape(8, C1, C2),
    )


def solution(mesh):
    return jax.shard_map(
        local,
        mesh=mesh,
        in_specs=(
            P("gx", "gy", None, None, None),
            P("gx", "gy", None, None),
            P("gx", "gy", None, None),
            P(),
            P(),
            P("gx", "gy", None, None, None),
        ),
        out_specs=(P("gx", "gy", None, None, None), P("gx", "gy", None, None, None), P(), P()),
        check_vma=False,
    )
```

```python
import functools
import math

import jax
import jax.numpy as jnp
from jax import lax
from jax.experimental import pallas as pl
from jax.experimental.pallas import tpu as pltpu
from jax.sharding import PartitionSpec as P

MESH = pl.DeviceIdType.MESH
C1 = 128
C2 = 256
V = 512
X_LO, X_HI, RING = 2, 2, 8
NX = X_LO * X_HI

DOWN_PARTS, SUB_PARTS = 1, 2
SUB_OWNERS = RING - 1
SUB_T = -(-108 // (SUB_PARTS * NX * SUB_OWNERS))
SUB_PART = NX * SUB_OWNERS * SUB_T
SUB = SUB_PARTS * SUB_PART
DOWN_PART = 64 // DOWN_PARTS
HALF = SUB + 64
ORDER = (2, 1, 3, 0) if NX == 4 else (1, 0)
PARTS = [
    (SUB + i * DOWN_PART, RING, DOWN_PART // (NX * RING)) for i in range(DOWN_PARTS)
] + [(i * SUB_PART, SUB_OWNERS, SUB_T) for i in range(SUB_PARTS)]


FACES = ((1, 0), (-1, 0), (0, 1), (0, -1))
EDGES = ((1, 1), (1, -1), (-1, 1), (-1, -1))

F32 = jnp.float32
BF16 = jnp.bfloat16


def field_slabs(source, minus, zero, plus):
    place = lax.broadcasted_iota(jnp.int32, (1, 8, C1), 1)
    below = jnp.where(place == 0, minus, zero)
    above = jnp.where(place == 7, plus, zero)
    return (
        pltpu.roll(source, 1, axis=1) * below,
        source * zero,
        pltpu.roll(source, 7, axis=1) * above,
    )


def kernel(
    near_in, feat_in, occ_in, wsub_in, wdown_in, cot_in,
    out_ref, gfeat_ref, gsum_ref,
    near_ref, feat_ref, occ_ref, wsub_ref, wdown_ref, cot_ref,
    mask_ref, shuf_ref, field_ref, cols_ref, wflip_ref, kids_ref,
    shalo, rhalo, g32, g16, in_sem, hs_sem, hr_sem, *part_refs,
):
    loads = [
        pltpu.make_async_copy(src, dst, in_sem.at[i])
        for i, (src, dst) in enumerate(
            (
                (occ_in, occ_ref), (feat_in, feat_ref), (near_in, near_ref),
                (wdown_in, wdown_ref), (cot_in, cot_ref), (wsub_in, wsub_ref),
            )
        )
    ]
    gx, gy = lax.axis_index("gx"), lax.axis_index("gy")
    core = gx % 2
    y = (gx // 2) % RING
    x = (gy % X_HI) * X_LO + gx // (2 * RING)
    z = gy // X_HI

    def device(px, py, pz, pc):
        return ((px % X_LO) * (2 * RING) + py * 2 + pc, pz * X_HI + px // X_LO)

    pa = jnp.where(core == 0, y, z)
    pb = jnp.where(core == 0, z, y)

    def on_plane(px, p):
        return device(px, jnp.where(core == 0, p, y), jnp.where(core == 0, z, p), core)

    def on_b(p):
        return device(x, jnp.where(core == 0, y, p), jnp.where(core == 0, p, z), core)

    partner = device(x, y, z, 1 - core)
    tiles_x, tiles_y = 2 * RING * X_LO, RING * X_HI

    def tile_at(dx, dy):
        return ((gx + dx + tiles_x) % tiles_x, (gy + dy + tiles_y) % tiles_y)

    places = [(pa + d) % RING for d in range(RING)]
    barrier = pltpu.get_barrier_semaphore()

    def greet(target):
        pl.semaphore_signal(barrier, inc=1, device_id=target, device_id_type=MESH)

    row = [jnp.where(core == 0, p, y) * 2 + core for p in places]
    column = [jnp.where(core == 0, z, p) * X_HI for p in places]
    x_low = [((x + dx) % NX) % X_LO * (2 * RING) for dx in range(NX)]
    x_high = [((x + dx) % NX) // X_LO for dx in range(NX)]
    plane = [(dx, d) for dx in range(NX) for d in range(RING) if dx or d]
    plane.sort(key=lambda step: -min(step[0], NX - step[0]) - min(step[1], RING - step[1]))

    def greet_plane(steps):
        for dx, d in steps:
            greet((x_low[dx] + row[d], column[d] + x_high[dx]))

    far = len(plane) * 2 // 5
    greet_plane(plane[:far])
    for dx, dy in EDGES + FACES:
        greet(tile_at(dx, dy))
    ring = [on_b((pb + d) % RING) for d in range(RING)]
    for d in range(1, RING):
        greet(ring[d])
    greet_plane(plane[far:])
    greet(partner)
    for load in loads:
        load.start()

    def remote(src, dst, send, recv, target):
        return pltpu.make_async_remote_copy(
            src_ref=src, dst_ref=dst, send_sem=send, recv_sem=recv,
            device_id=target, device_id_type=MESH,
        )

    def send_halo(which):
        for d, (dx, dy) in enumerate(EDGES):
            region = pl.ds(16 + d, 1)
            remote(shalo.at[which, region], rhalo.at[which, region], hs_sem.at[which],
                   hr_sem.at[which], tile_at(dx, dy)).start()
        for d, (dx, dy) in reversed(list(enumerate(FACES))):
            region = pl.ds(4 * d, 4)
            remote(shalo.at[which, region], rhalo.at[which, region], hs_sem.at[which],
                   hr_sem.at[which], tile_at(dx, dy)).start()

    def whole_halo(which):
        return remote(shalo.at[which], rhalo.at[which], hs_sem.at[which], hr_sem.at[which], partner)

    def stage_halo(which, value):
        cells = value.reshape(8, 8, 8, C1)
        side = {1: 7, -1: 0}
        for d, (dx, dy) in enumerate(FACES):
            face = cells[side[dx]] if dx else cells[:, side[dy]]
            shalo[which, 4 * d : 4 * d + 4] = face.reshape(4, 16, C1).astype(BF16)
        for d, (dx, dy) in enumerate(EDGES):
            edge = cells[side[dx], side[dy]]
            shalo[which, 16 + d] = jnp.concatenate([edge, edge], axis=0).astype(BF16)

    def named(dx, dy, d0, d1):
        return [
            jnp.where(near_ref[0, 9 * (d0 + 1) + 3 * (d1 + 1) + l] == 3 * (dx + 1) + dy + 1, 1.0, 0.0)
            for l in range(3)
        ]

    def center(value):
        slabs = field_slabs(value.reshape(64, 8, C1), F32(0.0), F32(1.0), F32(0.0))
        for l in range(3):
            field_ref[l, 1:9, 1:9] = slabs[l].reshape(8, 8, 8, C1)

    def columns(which):
        corner = {}

        def add_corner(cx, cy, slabs):
            for l in range(3):
                old = corner.get((cx, cy, l))
                corner[cx, cy, l] = slabs[l] if old is None else old + slabs[l]

        place = {1: 9, -1: 0}
        near_row = {1: 0, -1: 7}
        for dx, dy in FACES:
            slot = FACES.index((-dx, -dy))
            face = rhalo[which, 4 * slot : 4 * slot + 4].astype(F32).reshape(8, 8, C1)
            slabs = field_slabs(face, *named(dx, dy, dx, dy))
            for l in range(3):
                if dx:
                    field_ref[l, place[dx], 1:9] = slabs[l]
                else:
                    for r in range(8):
                        field_ref[l, 1 + r, place[dy]] = slabs[l][r]
            for side in (1, -1):
                row = near_row[side]
                d0, d1 = (dx, side) if dx else (side, dy)
                add_corner(
                    place[d0], place[d1],
                    field_slabs(face[row : row + 1], *named(dx, dy, d0, d1)),
                )
        for dx, dy in EDGES:
            slot = EDGES.index((-dx, -dy))
            edge = rhalo[which, 16 + slot].astype(F32)[0:8].reshape(1, 8, C1)
            add_corner(place[dx], place[dy], field_slabs(edge, *named(dx, dy, dx, dy)))
        for (cx, cy, l), slab in corner.items():
            field_ref[l, cx, cy] = slab[0]
        for i in range(3):
            for j in range(3):
                for l in range(3):
                    k = 9 * i + 3 * j + l
                    window = field_ref[l, i : i + 8, j : j + 8]
                    cols_ref[:, k * C1 : (k + 1) * C1] = window.reshape(V, C1).astype(BF16)

    def split_children(value):
        cells = value.reshape(8, 4, 2, 8, C1)
        for ey in range(2):
            shuf_ref[ey * 256 : (ey + 1) * 256] = cells[:, :, ey].reshape(256, C1)
        children = [None] * 8
        for ey in range(2):
            for ez in range(2):
                half = shuf_ref[pl.ds(ey * 256 + ez, 128, stride=2), :].reshape(4, 2, 16, C1)
                for ex in range(2):
                    children[4 * ex + 2 * ey + ez] = half[:, ex].reshape(64, C1)
        return children

    def join_children(children):
        for ey in range(2):
            for ez in range(2):
                pair = [children[4 * ex + 2 * ey + ez].reshape(4, 1, 16, C1) for ex in range(2)]
                shuf_ref[pl.ds(ey * 256 + ez, 128, stride=2), :] = jnp.concatenate(
                    pair, axis=1
                ).reshape(128, C1)
        sides = [shuf_ref[e * 256 : (e + 1) * 256].reshape(8, 4, 1, 8, C1) for e in range(2)]
        return jnp.concatenate(sides, axis=2).reshape(V, C1)

    loads[0].wait()
    for r in range(4):
        line = occ_ref[0:1, r * 128 : (r + 1) * 128].astype(F32)
        mask_ref[r * 128 : (r + 1) * 128] = jnp.broadcast_to(line, (128, 128)).T
    loads[1].wait()
    masked = feat_ref[...].astype(F32) * mask_ref[...]
    stage_halo(0, masked)
    pl.semaphore_wait(barrier, 9 + NX * RING - 1 + RING - 1)
    send_halo(0)

    center(masked)
    for load in loads[2:]:
        load.wait()
    for k in range(27):
        wflip_ref[:, k * C1 : (k + 1) * C1] = wsub_ref[(26 - k) * C1 : (27 - k) * C1]
    coarse = None
    for child in split_children(mask_ref[...]):
        coarse = child if coarse is None else jnp.maximum(coarse, child)
    coarse = jnp.concatenate([coarse, coarse], axis=1)
    seeded = (cot_ref[...].astype(F32) * coarse).astype(BF16)
    spread = lax.dot_general(
        seeded, wdown_ref[...], (((1,), (1,)), ((), ())), preferred_element_type=F32
    )
    hidden_grad = join_children([spread[:, r * C1 : (r + 1) * C1] for r in range(8)])

    whole_halo(0).wait_recv()
    columns(0)
    preact = jnp.dot(cols_ref[...], wsub_ref[...], preferred_element_type=F32)
    sig = jax.nn.sigmoid(preact)
    mask = mask_ref[...]
    hidden = (preact * sig * mask).astype(BF16).astype(F32)
    for r, child in enumerate(split_children(hidden)):
        kids_ref[:, r * C1 : (r + 1) * C1] = child.astype(BF16)

    mine, theirs = core * HALF, (1 - core) * HALF

    def put(tile, value):
        value = value.reshape(value.shape[0] // 16, 16, C1)
        g32[tile : tile + value.shape[0]] = value
        g16[tile : tile + value.shape[0]] = value.astype(BF16)

    class Part:
        def __init__(self, index):
            self.at, self.owners, self.t = PARTS[index]
            self.group = self.owners * self.t
            self.count = NX * self.group
            (self.rc, self.s16, self.r1, self.e,
             self.send, self.recv, self.late) = part_refs[7 * index : 7 * index + 7]

        def when_owner(self, body):
            if self.owners == RING:
                body()
            else:
                pl.when(pa < self.owners)(body)

        def unless_owner(self, body):
            if self.owners < RING:
                pl.when(pa >= self.owners)(body)

        def arrived(self, sem, region):
            remote(region, region, self.send.at[0], sem, partner).wait_recv()

        def left(self, which, tiles):
            region = gsum_ref.at[pl.ds(0, tiles)]
            remote(region, region, self.send.at[which], self.recv.at[0], partner).wait_send()

        def pair_sum(self, at, count):
            own = g32[pl.ds(mine + self.at + at, count)]
            return own + self.rc[pl.ds(at, count)].astype(F32)

        def core_start(self):
            remote(g16.at[pl.ds(theirs + self.at, self.count)], self.rc, self.send.at[0],
                   self.recv.at[0], partner).start()

        def scatter(self):
            self.arrived(self.recv.at[0], self.rc)
            self.s16[...] = self.pair_sum(0, self.count).astype(BF16)
            for dx in ORDER:
                px = (x + dx) % NX

                def body(i, carry):
                    p = (pa + RING // 2 + i) % RING

                    def start():
                        remote(self.s16.at[pl.ds((px * self.owners + p) * self.t, self.t)],
                               self.r1.at[(NX - dx) % NX * RING + pa], self.send.at[0],
                               self.recv.at[1], on_plane(px, p)).start()

                    if dx == 0:
                        pl.when((p < self.owners) & (p != pa))(start)
                    elif self.owners < RING:
                        pl.when(p < self.owners)(start)
                    else:
                        start()
                    return carry

                lax.fori_loop(0, RING, body, 0)

        def swap(self):
            def body():
                t = self.t
                self.arrived(self.recv.at[1], self.r1.at[pl.ds(1, NX * RING - 1)])
                self.r1[pa] = jnp.zeros((t, 16, C1), BF16)
                total = self.pair_sum((x * self.owners + pa) * t, t)
                for s in range(NX * RING):
                    total = total + self.r1[s].astype(F32)
                self.e[0] = total.astype(BF16)

                for s in sorted(range(1, RING), key=lambda s: -min(s, RING - s)):
                    remote(self.e.at[0], self.e.at[s], self.send.at[0], self.recv.at[2],
                           ring[s]).start()

            self.when_owner(body)

        def region(self, px, p, owners):
            return gsum_ref.at[pl.ds(mine + self.at + px * self.group + p * self.t, owners * self.t)]

        def gather(self):
            def body():
                self.arrived(self.recv.at[2], self.e.at[pl.ds(1, RING - 1)])
                total = self.e[pb % RING].astype(F32)
                for p in range(1, RING):
                    total = total + self.e[(pb - p + RING) % RING].astype(F32)
                own = self.region(x, pa, 1)
                own[...] = total.astype(BF16)
                for dx in ORDER:

                    def start(i, carry):
                        p = (pa + RING // 2 + i) % RING

                        def go():
                            remote(own, own, self.send.at[1], self.late.at[(NX - dx) % NX],
                                   on_plane((x + dx) % NX, p)).start()

                        if dx == 0:
                            pl.when(p != pa)(go)
                        else:
                            go()
                        return carry

                    lax.fori_loop(0, RING, start, 0)

            self.when_owner(body)

        def pass_on(self, g):
            px = (x + g) % NX
            whole = self.region(px, 0, self.owners)
            if g == 0:
                self.when_owner(
                    lambda: self.arrived(self.late.at[0], self.region(px, 0, self.owners - 1))
                )
                self.unless_owner(lambda: self.arrived(self.late.at[0], whole))
            else:
                self.arrived(self.late.at[g], whole)
            remote(whole, whole, self.send.at[1], self.recv.at[3], partner).start()

        def finish(self):
            self.arrived(self.recv.at[3], gsum_ref.at[pl.ds(theirs + self.at, self.count)])
            t, others = self.t, NX * RING - 1

            def owner():
                self.left(0, self.count + (NX * self.owners - 1 + RING - 1) * t)
                self.left(1, self.count + others * t)

            def rest():
                self.left(0, self.count + NX * self.owners * t)
                self.left(1, self.count)

            self.when_owner(owner)
            self.unless_owner(rest)

    parts = [Part(i) for i in range(DOWN_PARTS + SUB_PARTS)]
    split = DOWN_PARTS + SUB_PARTS // 2

    grad_down = lax.dot_general(
        kids_ref[...], seeded, (((0,), (0,)), ((), ())), preferred_element_type=F32
    )
    put(SUB, grad_down[:, :C1])
    put(HALF + SUB, grad_down[:, C1:])
    for part in parts[:DOWN_PARTS]:
        part.core_start()

    slope = sig * (1.0 + preact * (1.0 - sig))
    pre_grad = (hidden_grad * slope * mask).astype(BF16).astype(F32)
    turned = pre_grad.T.astype(BF16)

    def put_sub(low, high):
        blocks = jnp.dot(
            turned, cols_ref[:, low * C1 : high * C1], preferred_element_type=F32
        )
        for k in range(low, high):
            block = blocks[:, (k - low) * C1 : (k - low + 1) * C1].T
            if k < 13:
                put(8 * k, block)
            elif k == 13:
                put(8 * k, block[:64])
                put(HALF, block[64:])
            else:
                put(HALF + 8 * k - 108, block)

    early = SUB_PARTS // 2 * SUB_PART
    first = -(-early // 8)
    second = -(-(108 + early) // 8)
    put_sub(0, first)
    put_sub(13, second)
    for part in parts[DOWN_PARTS:split]:
        part.core_start()
    put_sub(first, 13)
    put_sub(second, 27)
    if SUB > 108:
        for h in range(2):
            put(h * HALF + 108, jnp.zeros(((SUB - 108) * 16, C1), F32))
    for part in parts[split:]:
        part.core_start()
    for part in parts:
        part.scatter()
    stage_halo(1, pre_grad)
    send_halo(1)

    for part in parts:
        part.swap()
    for part in parts:
        part.gather()

    center(pre_grad)
    whole_halo(1).wait_recv()
    columns(1)
    gfeat = lax.dot_general(
        cols_ref[...], wflip_ref[...], (((1,), (1,)), ((), ())), preferred_element_type=F32
    )
    gfeat_ref[...] = (gfeat * mask_ref[...]).astype(BF16)
    output = jnp.dot(kids_ref[...], wdown_ref[...], preferred_element_type=F32)
    out_ref[...] = (output * coarse).astype(BF16)

    for part in parts:
        for g in ORDER:
            part.pass_on(g)
    for part in parts:
        part.finish()
    for which in range(2):
        whole_halo(which).wait_send()


def finish_kernel(
    scale, sums_ref, output_ref, gfeat_ref, output, gfeat, gsub, gdown, sub_ref, down_ref, sem
):
    copies = []

    def store(src, dst):
        copies.append(pltpu.make_async_copy(src, dst, sem.at[len(copies)]))
        copies[-1].start()

    def widened(low, high):
        return (sums_ref[low:high].astype(F32) * scale).reshape(-1, C1)

    store(output_ref, output)
    store(gfeat_ref, gfeat)
    for h in range(2):
        for i in range(3):
            rows = pl.ds((h * 108 + i * 36) * 16, 36 * 16)
            sub_ref[rows] = widened(h * HALF + i * 36, h * HALF + i * 36 + 36)
            store(sub_ref.at[rows], gsub.at[rows])
    for r in range(2):
        rows = pl.ds(r * 512, 512)
        for h in range(2):
            low = h * HALF + SUB + r * 32
            down_ref[rows, h * C1 : (h + 1) * C1] = widened(low, low + 32)
        store(down_ref.at[rows], gdown.at[rows])
    for copy in copies:
        copy.wait()


def local(features, occupancy, neighbours, weight_sub, weight_down, cotangent):
    def tiles(*shape):
        return pltpu.VMEM(shape + (16, C1), BF16)

    vmem, any_space = pl.BlockSpec(memory_space=pltpu.VMEM), pl.BlockSpec(memory_space=pl.ANY)
    dma = pltpu.SemaphoreType.DMA
    part_scratch = []
    for _, owners, t in PARTS:
        count = NX * owners * t
        part_scratch += [
            tiles(count), tiles(count), tiles(NX * RING, t), tiles(RING, t),
            dma((2,)), dma((4,)), dma((NX,)),
        ]
    output, grad_features, sums = pl.pallas_call(
        kernel,
        out_shape=(
            pltpu.VMEM((64, C2), BF16), pltpu.VMEM((V, C1), BF16), tiles(2 * HALF),
        ),
        in_specs=[any_space] * 6,
        out_specs=(vmem,) * 3,
        scratch_shapes=[
            pltpu.SMEM((1, 27), jnp.int32),
            pltpu.VMEM((V, C1), BF16),
            pltpu.VMEM((1, V), jnp.int32),
            pltpu.VMEM((27 * C1, C1), BF16),
            pltpu.VMEM((8 * C1, C2), BF16),
            pltpu.VMEM((64, C2), BF16),
            pltpu.VMEM((V, C1), F32),
            pltpu.VMEM((V, C1), F32),
            pltpu.VMEM((3, 10, 10, 8, C1), F32),
            pltpu.VMEM((V, 27 * C1), BF16),
            pltpu.VMEM((C1, 27 * C1), BF16),
            pltpu.VMEM((64, 8 * C1), BF16),
            tiles(2, 20), tiles(2, 20),
            pltpu.VMEM((2 * HALF, 16, C1), F32),
            tiles(2 * HALF),
            dma((6,)), dma((2,)), dma((2,)),
        ] + part_scratch,
        compiler_params=pltpu.CompilerParams(
            collective_id=0, has_side_effects=True, vmem_limit_bytes=40 * 1024 * 1024
        ),
    )(
        *(
            pltpu.with_memory_space_constraint(arg, pltpu.HBM)
            for arg in (
                neighbours.reshape(1, 27),
                features.reshape(V, C1),
                occupancy.reshape(1, V),
                weight_sub.reshape(27 * C1, C1),
                weight_down.reshape(8 * C1, C2),
                cotangent.reshape(64, C2),
            )
        )
    )
    scale = 1.0 / math.sqrt(lax.axis_size("gx") * lax.axis_size("gy") * V)
    output, grad_features, grad_sub, grad_down = pl.pallas_call(
        functools.partial(finish_kernel, scale),
        out_shape=(
            jax.ShapeDtypeStruct((64, C2), BF16),
            jax.ShapeDtypeStruct((V, C1), BF16),
            jax.ShapeDtypeStruct((27 * C1, C1), F32),
            jax.ShapeDtypeStruct((8 * C1, C2), F32),
        ),
        in_specs=[vmem] * 3,
        out_specs=(any_space,) * 4,
        scratch_shapes=[
            pltpu.VMEM((27 * C1, C1), F32), pltpu.VMEM((8 * C1, C2), F32), dma((10,)),
        ],
        compiler_params=pltpu.CompilerParams(vmem_limit_bytes=16 * 1024 * 1024),
    )(sums, output, grad_features)
    return (
        output.reshape(1, 1, 1, 64, C2),
        grad_features.reshape(1, 1, 1, V, C1),
        grad_sub.reshape(27, C1, C1),
        grad_down.reshape(8, C1, C2),
    )


def solution(mesh):
    return jax.shard_map(
        local,
        mesh=mesh,
        in_specs=(
            P("gx", "gy", None, None, None),
            P("gx", "gy", None, None),
            P("gx", "gy", None, None),
            P(),
            P(),
            P("gx", "gy", None, None, None),
        ),
        out_specs=(P("gx", "gy", None, None, None), P("gx", "gy", None, None, None), P(), P()),
        check_vma=False,
    )
```
